128 devices in a mesh: prop: 16 (over z, x_hi, core), cross: 8 (over x_lo, y).
Axes of the slice: x: 4 (x_hi: 2, x_lo: 2; x = x_hi * 2 + x_lo), y: 4, z: 4, core: 2. Of those that a mesh axis runs over, the one named last changes fastest.
Arguments:
- gas: float32 [5, 64, 256, 512], P(None, 'prop', 'cross'), may hold values from -4 to 4
- parcel_state: float32 [2, 2097152], P(None, ('prop', 'cross')), may hold values from 0.5 to 2
- parcel_cell: int32 [2097152], P(('prop', 'cross')), may hold values from 0 to 65535
- parcel_dest: int32 [2097152], P(('prop', 'cross')), may hold values from 0 to 65535
- send_slot: int32 [2097152], P(('prop', 'cross')), may hold values from -1 to 4095, as said below
- face_counts: int32 [16, 8, 2], P('prop', 'cross'), may hold values from 0 to 2048, as said below
Outputs:
- gas_out: float32 [5, 64, 256, 512], P(None, 'prop', 'cross')
- parcels_out: float32 [2, 2097152], P(None, ('prop', 'cross'))
- arrivals: float32 [2, 3, 262144], P(None, None, ('prop', 'cross'))
The draws below stay inside these ranges and needn't reach their ends.
Inputs may be any that keep to these rules, and one draw needn't show every extreme that they name: face_counts[p, c, 0] and face_counts[p, c, 1] count the parcels that device (p, c) sends toward lower and higher propagation index; the devices of at most three adjacent slabs send 2048 through both faces, which is reached in every draw. `send_slot`: -1 for a parcel that stays; otherwise f * 2048 + j with face f (0 lower, 1 higher) and j below that device's face_counts for f; on each device every such code is used by exactly one parcel.
All inputs are finite; a program needn't handle non-finite values.
Results may differ from the reference program's by a relative error of at most 0.0003.
Values sent between devices are 32-bit elements; how exact they have to be, the bound alone decides.
A program may use at most 64 MiB of HBM per device.

```python
import jax
import jax.numpy as jnp

CX = 4
CY = 32
CZ = 512
P_DEV = 16384
SUBSTEPS = 2
CELLS = 65536
NX = 64
NY = 256
NP = 2097152
N_PROP = 16
N_CROSS = 8


def routing(key):
    slots = P_DEV // 8
    front_key, count_key, perm_key = jax.random.split(jax.random.fold_in(key, 7), 3)
    front = jax.random.randint(front_key, (), 0, N_PROP)
    prop_index = jnp.arange(N_PROP, dtype=jnp.int32)[:, None, None]
    near = jnp.abs(prop_index - front) <= 1
    base = slots // 8 + jax.random.randint(count_key, (N_PROP, N_CROSS, 2), 0, slots // 4)
    counts = jnp.where(near, slots, base).astype(jnp.int32)
    keys = jax.random.split(perm_key, N_PROP * N_CROSS)
    orders = jax.vmap(lambda k: jax.random.permutation(k, P_DEV))(keys).reshape(N_PROP, N_CROSS, P_DEV)
    rank = jnp.arange(P_DEV, dtype=jnp.int32)[None, None, :]
    lower = counts[:, :, 0:1]
    upper = counts[:, :, 1:2]
    code = jnp.where(rank < lower, rank, jnp.where(rank < lower + upper, slots + rank - lower, -1)).astype(jnp.int32)

    def place(order, codes):
        return jnp.zeros((P_DEV,), jnp.int32).at[order].set(codes)
    slot = jax.vmap(jax.vmap(place))(orders, code)
    return (counts, slot.reshape(N_PROP * N_CROSS * P_DEV))


def draw_face_counts(key, part):
    return routing(key)[0]


def draw_send_slot(key, part):
    return routing(key)[1]


def plant(entries, stream_key, smallest, high):
    longest = entries.shape.index(max(entries.shape))
    spots = []
    for shift in (0, 1):
        where = [jax.random.randint(jax.random.fold_in(stream_key, axis), (), 0, length) for axis, length in enumerate(entries.shape)]
        where[longest] = (where[longest] + shift) % entries.shape[longest]
        spots.append(tuple(where))
    return entries.at[spots[0]].set(smallest).at[spots[1]].set(high)


def steps_of(key, extent, pieces, low, top_value):
    def one(position, parts):
        draws = jax.random.uniform(jax.random.fold_in(jax.random.fold_in(key, 6), position), (parts,), jnp.float32, low / len(pieces), top_value / len(pieces))
        return jnp.repeat(jnp.exp(draws), extent[position] // parts).reshape((-1,) + (1,) * (len(extent) - position - 1))

    factor_of = one(*pieces[0])
    for cut in pieces[1:]:
        factor_of = factor_of * one(*cut)
    return factor_of


def gaussian(own_key, dims, deviation, bound, shards=(), kind=jnp.bfloat16):
    array = deviation * jax.random.normal(own_key, dims, jnp.float32)
    if shards:
        array = array * steps_of(own_key, dims, shards, -0.22, 0.18)
    return jnp.clip(array, -bound, bound).astype(kind)


def setup_inputs(seed: int = 0) -> dict:
    key_list = jax.random.split(jax.random.key(seed), 7)
    gas = gaussian(key_list[0], (5, NX, NY, CZ), 1.0, 4.0, ((1, 16), (2, 8)), jnp.float32)
    parcel_state = jnp.clip(0.5 + 1.5 * jax.random.uniform(key_list[1], (2, NP), jnp.float32) ** steps_of(key_list[1], (2, NP), ((1, 128),), -0.2, 0.2), 0.5, 2.0)
    parcel_cell = plant(jax.random.randint(key_list[2], (NP,), 0, CELLS), jax.random.fold_in(key_list[2], 1), 0, CELLS - 1).astype(jnp.int32)
    parcel_dest = plant(jax.random.randint(key_list[3], (NP,), 0, CELLS), jax.random.fold_in(key_list[3], 1), 0, CELLS - 1).astype(jnp.int32)
    send_slot = draw_send_slot(jax.random.fold_in(key_list[6], 71), 0)
    face_counts = draw_face_counts(jax.random.fold_in(key_list[6], 71), 0)
    return dict(gas=gas, parcel_state=parcel_state, parcel_cell=parcel_cell, parcel_dest=parcel_dest, send_slot=send_slot, face_counts=face_counts)


def advance(padded):
    zpad = jnp.pad(padded, ((0, 0), (0, 0), (0, 0), (1, 1)))
    center = zpad[:, 1:-1, 1:-1, 1:-1]
    xplus = zpad[:, 2:, 1:-1, 1:-1]
    xminus = zpad[:, :-2, 1:-1, 1:-1]
    yplus = zpad[:, 1:-1, 2:, 1:-1]
    yminus = zpad[:, 1:-1, :-2, 1:-1]
    zplus = zpad[:, 1:-1, 1:-1, 2:]
    zminus = zpad[:, 1:-1, 1:-1, :-2]
    carry_x = center[0:1]
    carry_y = center[1:2]
    carry_z = center[2:3]
    advect = 0.5 * (carry_x * (xplus - xminus) + carry_y * (yplus - yminus) + carry_z * (zplus - zminus))
    laplace = xplus + xminus + yplus + yminus + zplus + zminus - 6.0 * center
    fresh = center - 0.1 * advect + 0.12 * laplace
    return fresh.at[2].add(0.1 * center[3])


def burn(state, seen):
    mass = state[0]
    temper = state[1]
    hot = temper + 0.3 * (seen - temper)
    burned = 0.2 * mass * (1.0 + 0.5 * jnp.tanh(hot))
    return jnp.stack([mass - burned, hot + 0.5 * burned, burned], axis=0)


def make_buffers(records, dest, slot, counts, slots):
    index = jnp.where(slot >= 0, slot, 2 * slots).astype(jnp.int32)
    rec_buf = jnp.zeros((3, 2 * slots + 1), records.dtype).at[:, index].set(records)[:, :2 * slots]
    rec_buf = rec_buf.reshape(3, 2, slots).transpose(1, 0, 2)
    dest_buf = jnp.zeros((2 * slots + 1,), jnp.int32).at[index].set(dest)[:2 * slots].reshape(2, slots)
    live = jnp.arange(slots, dtype=jnp.int32)[None, :] < counts[:, None]
    rec_buf = jnp.where(live[:, None, :], rec_buf, jnp.zeros_like(rec_buf))
    dest_buf = jnp.where(live, dest_buf, jnp.zeros_like(dest_buf))
    return rec_buf, dest_buf


def deposit(burned, slot, dest, arr_burn, arr_dest, ncell):
    stay = slot < 0
    total = jnp.zeros((ncell,), burned.dtype).at[dest].add(jnp.where(stay, burned, jnp.zeros_like(burned)))
    return total.at[arr_dest.reshape(-1)].add(arr_burn.reshape(-1))


def reference(gas, parcel_state, parcel_cell, parcel_dest, send_slot, face_counts):
    settled = gas
    for step in range(SUBSTEPS):
        settled = advance(jnp.pad(settled, ((0, 0), (1, 1), (1, 1), (0, 0))))
    ncell = CX * CY * CZ
    blocks = settled.reshape(5, N_PROP, CX, N_CROSS, CY, CZ).transpose(1, 3, 0, 2, 4, 5).reshape(N_PROP, N_CROSS, 5, ncell)
    state = parcel_state.reshape(2, N_PROP, N_CROSS, P_DEV).transpose(1, 2, 0, 3)
    cell = parcel_cell.reshape(N_PROP, N_CROSS, P_DEV)
    dest = parcel_dest.reshape(N_PROP, N_CROSS, P_DEV)
    slot = send_slot.reshape(N_PROP, N_CROSS, P_DEV)
    seen = jnp.take_along_axis(blocks[:, :, 3, :], cell, axis=2)
    records = jax.vmap(jax.vmap(burn))(state, seen)
    slots = P_DEV // 8
    builder = jax.vmap(jax.vmap(lambda r, d, s, c: make_buffers(r, d, s, c, slots)))
    rec_buf, dest_buf = builder(records, dest, slot, face_counts)
    from_below = jnp.concatenate([jnp.zeros_like(rec_buf[:1, :, 1]), rec_buf[:-1, :, 1]], axis=0)
    from_above = jnp.concatenate([rec_buf[1:, :, 0], jnp.zeros_like(rec_buf[:1, :, 0])], axis=0)
    dest_below = jnp.concatenate([jnp.zeros_like(dest_buf[:1, :, 1]), dest_buf[:-1, :, 1]], axis=0)
    dest_above = jnp.concatenate([dest_buf[1:, :, 0], jnp.zeros_like(dest_buf[:1, :, 0])], axis=0)
    arrived = jnp.stack([from_below, from_above], axis=2)
    arrived_dest = jnp.stack([dest_below, dest_above], axis=2)
    spread = jax.vmap(jax.vmap(lambda b, s, d, ab, ad: deposit(b, s, d, ab, ad, ncell)))
    release = spread(records[:, :, 2], slot, dest, arrived[:, :, :, 2], arrived_dest)
    blocks = blocks.at[:, :, 3].add(1.5 * release)
    blocks = blocks.at[:, :, 4].add(release)
    gas_out = blocks.reshape(N_PROP, N_CROSS, 5, CX, CY, CZ).transpose(2, 0, 3, 1, 4, 5).reshape(5, N_PROP * CX, N_CROSS * CY, CZ)
    parcels_out = records[:, :, :2].transpose(2, 0, 1, 3).reshape(2, N_PROP * N_CROSS * P_DEV)
    arrivals = arrived.transpose(2, 3, 0, 1, 4).reshape(2, 3, N_PROP * N_CROSS * slots)
    return gas_out, parcels_out, arrivals
```

```python
import jax
import jax.numpy as jnp
from jax import lax
from jax.experimental import pallas as pl
from jax.experimental.pallas import tpu as pltpu
from jax.sharding import PartitionSpec as P
F32=jnp.float32; BF=jnp.bfloat16

def iota_bf(n):
    return lax.broadcasted_iota(jnp.int32,(n,128),0).astype(F32).astype(BF)

def wide(row, n):
    t = jnp.broadcast_to(row,(16,128)).astype(BF)
    return jnp.concatenate([t]*(n//16),axis=0)

def split(x):
    hi = x.astype(BF).astype(F32)
    return hi, x-hi

def table(T, tab_ref):
    hi, lo = split(T)
    m = jnp.concatenate([hi[:, :256], hi[:, 256:], lo[:, :256], lo[:, 256:]], axis=0)
    tab_ref[...] = m.T.astype(BF)

def gather_block(b, rows, mode, cell_ref, tab_ref, seen_ref):
    cell = cell_ref[pl.ds(pl.multiple_of(b*rows,8), rows), :]
    key = (((cell >> 8) & 1) * 128 + (cell >> 9)).astype(F32)
    lo = (cell & 255).astype(F32)
    it = iota_bf(256)
    one = jnp.ones((256,128),BF); zero=jnp.zeros((256,128),BF)
    oh = jnp.concatenate([jnp.where(it == wide(key[i:i+1],256), one, zero) for i in range(rows)],axis=1)
    if mode == 0:
        res = jnp.dot(tab_ref[...], jnp.concatenate([oh,oh],axis=0), preferred_element_type=F32)
    else:
        res = jnp.dot(tab_ref[:, :256], oh, preferred_element_type=F32) + jnp.dot(tab_ref[:, 256:], oh, preferred_element_type=F32)
    itf = lax.broadcasted_iota(jnp.int32,(256,128),0).astype(F32)
    out = []
    for i in range(rows):
        r = res[:, i*128:(i+1)*128]
        out.append(jnp.sum(jnp.where(itf == lo[i:i+1], r, 0.0),axis=0,keepdims=True))
    seen_ref[pl.ds(pl.multiple_of(b*rows,8), rows), :] = jnp.concatenate(out,axis=0)

def burn_all(state_ref, seen, slot, out_ref, rec_ref):
    mass = state_ref[pl.ds(0,128,stride=2),:]
    temper = state_ref[pl.ds(1,128,stride=2),:]
    hot = temper + 0.3*(seen-temper)
    burned = 0.2*mass*(1.0+0.5*jnp.tanh(hot))
    left = mass-burned
    warm = hot+0.5*burned
    out_ref[pl.ds(0,128,stride=2),:] = left
    out_ref[pl.ds(1,128,stride=2),:] = warm
    rec_ref[0]=left; rec_ref[1]=warm; rec_ref[2]=burned

NT=(((1,),(1,)),((),()))

def compact_block(b, rows, slot_ref, dest_ref, rec_ref, acc_ref):
    ds = pl.ds(pl.multiple_of(b*rows,8), rows)
    slot = slot_ref[ds,:]; dest = dest_ref[ds,:]
    hi = (slot>>8).astype(F32); lo=(slot&255).astype(F32)
    vals=[]
    for f in range(3):
        vals += list(split(rec_ref[f, ds, :]))
    vals += [(dest>>8).astype(F32), (dest&255).astype(F32)]
    it = iota_bf(256); it16 = iota_bf(16)
    one = jnp.ones((256,128),BF); zero=jnp.zeros((256,128),BF)
    z16=jnp.zeros((16,128),BF)
    As=[];Bs=[]
    for i in range(rows):
        Bs.append(jnp.where(it == wide(lo[i:i+1],256), one, zero))
        m = it16 == wide(hi[i:i+1],16)
        As.append(jnp.concatenate([jnp.where(m, wide(v[i:i+1],16), z16) for v in vals],axis=0))
    A=jnp.concatenate(As,axis=1); B=jnp.concatenate(Bs,axis=1)
    acc_ref[...] += lax.dot_general(A,B,NT,preferred_element_type=F32)

def deposit_block(dest, burned, rows, acc_ref):
    hi=(((dest >> 8) & 1) * 128 + (dest >> 9)).astype(F32); lo=(dest&255).astype(F32)
    bh, bl = split(burned)
    it = iota_bf(256)
    one = jnp.ones((256,128),BF); zero=jnp.zeros((256,128),BF)
    As=[];Bs=[]
    for i in range(rows):
        Bs.append(jnp.where(it == wide(lo[i:i+1],256), one, zero))
        m = it == wide(hi[i:i+1],256)
        As.append(jnp.concatenate([jnp.where(m, wide(bh[i:i+1],256), zero),jnp.where(m, wide(bl[i:i+1],256), zero)],axis=0))
    A=jnp.concatenate(As,axis=1); B=jnp.concatenate(Bs,axis=1)
    acc_ref[...] += lax.dot_general(A,B,NT,preferred_element_type=F32)


def padded_2(x, sides, width):
    for axis, dim in sides:
        devices, length = (lax.axis_size(axis), x.shape[dim])
        up = [(i, (i + 1) % devices) for i in range(devices - 1)]
        down = [(j, i) for i, j in up]
        last = lax.slice_in_dim(x, length - width, length, axis=dim)
        initial = lax.slice_in_dim(x, 0, width, axis=dim)
        before = lax.ppermute(last, axis, up)
        after = lax.ppermute(initial, axis, down)
        x = jnp.concatenate([before, x, after], axis=dim)
    return x


def shifted(block, axis, distance):
    devices = range(lax.axis_size(axis))
    route = [(i - distance, i) for i in devices if i - distance in devices]
    return lax.ppermute(block, axis, route)


def advance(padded):
    zpad = jnp.pad(padded, ((0, 0), (0, 0), (0, 0), (1, 1)))
    center = zpad[:, 1:-1, 1:-1, 1:-1]
    xplus = zpad[:, 2:, 1:-1, 1:-1]
    xminus = zpad[:, :-2, 1:-1, 1:-1]
    yplus = zpad[:, 1:-1, 2:, 1:-1]
    yminus = zpad[:, 1:-1, :-2, 1:-1]
    zplus = zpad[:, 1:-1, 1:-1, 2:]
    zminus = zpad[:, 1:-1, 1:-1, :-2]
    carry_x = center[0:1]
    carry_y = center[1:2]
    carry_z = center[2:3]
    advect = 0.5 * (
        carry_x * (xplus - xminus) + carry_y * (yplus - yminus) + carry_z * (zplus - zminus)
    )
    laplace = xplus + xminus + yplus + yminus + zplus + zminus - 6.0 * center
    fresh = center - 0.1 * advect + 0.12 * laplace
    return fresh.at[2].add(0.1 * center[3])


SUBSTEPS = 2
ROWS = 16
VM = pl.BlockSpec(memory_space=pltpu.VMEM)


def parcels_kernel(temp_ref, cell_ref, dest_ref, slot_ref, state_ref, out_ref, box_ref, rel_ref, tab, seen, rec, acc):
    table(temp_ref[...], tab)
    steps = 128 // ROWS

    def gather(b, c):
        gather_block(b, ROWS, 1, cell_ref, tab, seen)
        return c
    lax.fori_loop(0, steps, gather, 0)
    burn_all(state_ref, seen[...], slot_ref[...], out_ref, rec)
    acc[...] = jnp.zeros_like(acc)

    def compact(b, c):
        compact_block(b, ROWS, slot_ref, dest_ref, rec, acc)
        return c
    lax.fori_loop(0, steps, compact, 0)
    for f in range(4):
        first, second = acc[32 * f:32 * f + 16, :], acc[32 * f + 16:32 * f + 32, :]
        both = first * 256.0 + second if f == 3 else first + second
        box_ref[0, f] = both[:8]
        box_ref[1, f] = both[8:]
    rel_ref[...] = jnp.zeros_like(rel_ref)

    def deposit(b, c):
        ds = pl.ds(pl.multiple_of(b * ROWS, 8), ROWS)
        burned = jnp.where(slot_ref[ds, :] < 0, rec[2, ds, :], 0.0)
        deposit_block(dest_ref[ds, :], burned, ROWS, rel_ref)
        return c
    lax.fori_loop(0, steps, deposit, 0)


def finish_kernel(low_ref, high_ref, rel_ref, gas_ref, out_ref, acc):
    acc[...] = rel_ref[...]
    for ref in (low_ref, high_ref):
        dest = ref[3].astype(jnp.int32)
        burned = jnp.concatenate([ref[2][:, :128], ref[2][:, 128:]], axis=0)
        dest = jnp.concatenate([dest[:, :128], dest[:, 128:]], axis=0)
        deposit_block(dest, burned, 16, acc)
    both = acc[:256, :] + acc[256:, :]
    release = jnp.concatenate([both[:128], both[128:]], axis=1).reshape(4, 32, 512)
    out_ref[0:3] = gas_ref[0:3]
    out_ref[3] = gas_ref[3] + 1.5 * release
    out_ref[4] = gas_ref[4] + release


def on_device(gas, parcel_state, parcel_cell, parcel_dest, send_slot, face_counts):
    rows, cols, depth = gas.shape[1:]
    settled = gas
    for step in range(SUBSTEPS):
        padded = padded_2(settled, (("prop", 1), ("cross", 2)), 1)
        settled = advance(padded)
    square = lambda a: a.reshape(128, 128)
    state = parcel_state.reshape(2, 128, 128).transpose(1, 0, 2).reshape(256, 128)
    params = pltpu.CompilerParams(vmem_limit_bytes=40 << 20)
    out, box, rel = pl.pallas_call(
        parcels_kernel,
        out_shape=(jax.ShapeDtypeStruct((256, 128), F32), jax.ShapeDtypeStruct((2, 4, 8, 256), F32), jax.ShapeDtypeStruct((512, 256), F32)),
        in_specs=[VM] * 5, out_specs=(VM, VM, VM),
        scratch_shapes=[pltpu.VMEM((256, 512), BF), pltpu.VMEM((128, 128), F32), pltpu.VMEM((3, 128, 128), F32), pltpu.VMEM((128, 256), F32)],
        compiler_params=params, name="parcels",
    )(settled[3].reshape(128, 512), square(parcel_cell), square(parcel_dest), square(send_slot), state)
    parcels_out = out.reshape(128, 2, 128).transpose(1, 0, 2).reshape(2, 16384)
    slots = 2048
    counts = face_counts.reshape(2)
    live = jnp.arange(slots, dtype=jnp.int32).reshape(8, 256)[None] < counts[:, None, None]
    box = jnp.where(live[:, None], box, 0.0)
    low = shifted(box[1], "prop", 1)
    high = shifted(box[0], "prop", -1)
    gas_out = pl.pallas_call(
        finish_kernel, out_shape=jax.ShapeDtypeStruct(gas.shape, F32),
        in_specs=[VM] * 4, out_specs=VM, scratch_shapes=[pltpu.VMEM((512, 256), F32)],
        compiler_params=params, name="finish",
    )(low, high, rel, settled)
    arrivals = jnp.stack([low[:3].reshape(3, slots), high[:3].reshape(3, slots)], axis=0)
    return (gas_out, parcels_out, arrivals)


def solution(mesh):
    in_specs = (
        P(None, "prop", "cross", None),
        P(None, ("prop", "cross")),
        P(("prop", "cross")),
        P(("prop", "cross")),
        P(("prop", "cross")),
        P("prop", "cross", None),
    )
    out_specs = (
        P(None, "prop", "cross", None),
        P(None, ("prop", "cross")),
        P(None, None, ("prop", "cross")),
    )
    return jax.shard_map(
        on_device, mesh=mesh, in_specs=in_specs, out_specs=out_specs, check_vma=False
    )
```

```python
import functools
import jax
import jax.numpy as jnp
from jax import lax
from jax.experimental import pallas as pl
from jax.experimental.pallas import tpu as pltpu
from jax.sharding import PartitionSpec as P

F32 = jnp.float32
BF = jnp.bfloat16
ROWS = 16
NT = (((1,), (1,)), ((), ()))
GROUPS = ((3, 4), (0, 3), (4, 5))


def iota_bf(n):
    return lax.broadcasted_iota(jnp.int32, (n, 128), 0).astype(F32).astype(BF)


def wide(row, n):
    t = jnp.broadcast_to(row, (16, 128)).astype(BF)
    return jnp.concatenate([t] * (n // 16), axis=0)


def split(x):
    hi = x.astype(BF).astype(F32)
    return hi, x - hi


def key_of(cell):
    return (((cell >> 8) & 1) * 128 + (cell >> 9)).astype(F32)


def low_of(cell):
    return (cell & 255).astype(F32)


def table(T, tab_ref):
    hi, lo = split(T)
    m = jnp.concatenate([hi[:, :256], hi[:, 256:], lo[:, :256], lo[:, 256:]], axis=0)
    tab_ref[...] = m.T.astype(BF)


def gather_block(b, rows, cell_ref, tab_ref, seen_ref):
    cell = cell_ref[pl.ds(pl.multiple_of(b * rows, 8), rows), :]
    key = key_of(cell)
    lo = low_of(cell)
    it = iota_bf(256)
    one = jnp.ones((256, 128), BF)
    zero = jnp.zeros((256, 128), BF)
    oh = jnp.concatenate([jnp.where(it == wide(key[i:i + 1], 256), one, zero) for i in range(rows)], axis=1)
    res = jnp.dot(tab_ref[:, :256], oh, preferred_element_type=F32) + jnp.dot(tab_ref[:, 256:], oh, preferred_element_type=F32)
    itf = lax.broadcasted_iota(jnp.int32, (256, 128), 0).astype(F32)
    out = []
    for i in range(rows):
        r = res[:, i * 128:(i + 1) * 128]
        out.append(jnp.sum(jnp.where(itf == lo[i:i + 1], r, 0.0), axis=0, keepdims=True))
    seen_ref[pl.ds(pl.multiple_of(b * rows, 8), rows), :] = jnp.concatenate(out, axis=0)


def burn_all(state_ref, seen, out_ref, rec_ref):
    mass = state_ref[pl.ds(0, 128, stride=2), :]
    temper = state_ref[pl.ds(1, 128, stride=2), :]
    hot = temper + 0.3 * (seen - temper)
    burned = 0.2 * mass * (1.0 + 0.5 * jnp.tanh(hot))
    left = mass - burned
    warm = hot + 0.5 * burned
    out_ref[pl.ds(0, 128, stride=2), :] = left
    out_ref[pl.ds(1, 128, stride=2), :] = warm
    rec_ref[0] = left
    rec_ref[1] = warm
    rec_ref[2] = burned


def compact_block(b, rows, slot_ref, dest_ref, rec_ref, acc_ref):
    ds = pl.ds(pl.multiple_of(b * rows, 8), rows)
    slot = slot_ref[ds, :]
    dest = dest_ref[ds, :]
    hi = (slot >> 8).astype(F32)
    lo = (slot & 255).astype(F32)
    vals = []
    for f in range(3):
        vals += list(split(rec_ref[f, ds, :]))
    vals += [(dest >> 8).astype(F32), (dest & 255).astype(F32)]
    it = iota_bf(256)
    it16 = iota_bf(16)
    one = jnp.ones((256, 128), BF)
    zero = jnp.zeros((256, 128), BF)
    z16 = jnp.zeros((16, 128), BF)
    As, Bs = [], []
    for i in range(rows):
        Bs.append(jnp.where(it == wide(lo[i:i + 1], 256), one, zero))
        m = it16 == wide(hi[i:i + 1], 16)
        As.append(jnp.concatenate([jnp.where(m, wide(v[i:i + 1], 16), z16) for v in vals], axis=0))
    A = jnp.concatenate(As, axis=1)
    B = jnp.concatenate(Bs, axis=1)
    acc_ref[...] += lax.dot_general(A, B, NT, preferred_element_type=F32)


def deposit_block(dest, burned, rows, acc_ref):
    hi = key_of(dest)
    lo = low_of(dest)
    bh, bl = split(burned)
    it = iota_bf(256)
    one = jnp.ones((256, 128), BF)
    zero = jnp.zeros((256, 128), BF)
    As, Bs = [], []
    for i in range(rows):
        Bs.append(jnp.where(it == wide(lo[i:i + 1], 256), one, zero))
        m = it == wide(hi[i:i + 1], 256)
        As.append(jnp.concatenate([jnp.where(m, wide(bh[i:i + 1], 256), zero), jnp.where(m, wide(bl[i:i + 1], 256), zero)], axis=0))
    A = jnp.concatenate(As, axis=1)
    B = jnp.concatenate(Bs, axis=1)
    acc_ref[...] += lax.dot_general(A, B, NT, preferred_element_type=F32)


def plane(g, hy, f, i):
    c = g[f, i]
    rows, depth = c.shape
    row = lax.broadcasted_iota(jnp.int32, (rows, depth), 0)
    lane = lax.broadcasted_iota(jnp.int32, (rows, depth), 1)
    xm, xp = g[f, i - 1], g[f, i + 1]
    ym = jnp.where(row == 0, hy[f, 0, pl.ds(i - 1, 1), :], pltpu.roll(c, 1, 0))
    yp = jnp.where(row == rows - 1, hy[f, 1, pl.ds(i - 1, 1), :], pltpu.roll(c, rows - 1, 0))
    zm = jnp.where(lane == 0, 0.0, pltpu.roll(c, 1, 1))
    zp = jnp.where(lane == depth - 1, 0.0, pltpu.roll(c, depth - 1, 1))
    advect = g[0, i] * (xp - xm) + g[1, i] * (yp - ym) + g[2, i] * (zp - zm)
    laplace = (xp + xm) + (yp + ym) + (zp + zm) - 6.0 * c
    return c - 0.05 * advect + 0.12 * laplace


def step_kernel(gas_hbm, cell_hbm, dest_hbm, slot_hbm, state_hbm, counts_ref,
                gas_out, state_out, arr_out,
                g0, g1, t2, hy0, hy1, sy0, sy1, cell, dest, slot, state,
                tab, seen, rec, acc, rel, box, got,
                in_sem, xs, xr, ys, yr, fs, fr):
    p, c = lax.axis_index("prop"), lax.axis_index("cross")
    np_, nc = lax.axis_size("prop"), lax.axis_size("cross")
    below = {"prop": lax.rem(p + np_ - 1, np_)}
    above = {"prop": lax.rem(p + 1, np_)}
    left = {"cross": lax.rem(c + nc - 1, nc)}
    right = {"cross": lax.rem(c + 1, nc)}
    gs, hys, sys_ = (g0, g1), (hy0, hy1), (sy0, sy1)

    def remote(a, b, s, r, to):
        return pltpu.make_async_remote_copy(src_ref=a, dst_ref=b, send_sem=s, recv_sem=r, device_id=to, device_id_type=pl.DeviceIdType.MESH)

    def halo(r, k):
        lo, hi = GROUPS[k]
        fields = pl.ds(lo, hi - lo)
        if r == 0:
            first, last = gas_hbm.at[fields, 0], gas_hbm.at[fields, 3]
        else:
            first, last = g1.at[fields, 1], g1.at[fields, 4]
        sy, hy, g = sys_[r], hys[r], gs[r]
        return [
            remote(first, g.at[fields, 5], xs.at[r, k, 0], xr.at[r, k, 0], below),
            remote(last, g.at[fields, 0], xs.at[r, k, 1], xr.at[r, k, 1], above),
            remote(sy.at[fields, 0], hy.at[fields, 1], ys.at[r, k, 0], yr.at[r, k, 0], left),
            remote(sy.at[fields, 1], hy.at[fields, 0], ys.at[r, k, 1], yr.at[r, k, 1], right),
        ]

    def stage(r, f):
        for i in range(4):
            sys_[r][f, 0, i:i + 1, :] = gs[r][f, 1 + i, 0:1, :]
            sys_[r][f, 1, i:i + 1, :] = gs[r][f, 1 + i, 31:32, :]

    def send(r, k):
        for copy in halo(r, k):
            copy.start()

    def receive(r, k):
        for copy in halo(r, k):
            copy.wait_recv()
        lo, hi = GROUPS[k]

        @pl.when(p == 0)
        def _():
            for f in range(lo, hi):
                gs[r][f, 0] = jnp.zeros((32, 512), F32)

        @pl.when(p == np_ - 1)
        def _():
            for f in range(lo, hi):
                gs[r][f, 5] = jnp.zeros((32, 512), F32)

        @pl.when(c == 0)
        def _():
            for f in range(lo, hi):
                hys[r][f, 0] = jnp.zeros((4, 512), F32)

        @pl.when(c == nc - 1)
        def _():
            for f in range(lo, hi):
                hys[r][f, 1] = jnp.zeros((4, 512), F32)

    loads = [
        pltpu.make_async_copy(gas_hbm.at[pl.ds(3, 1)], g0.at[pl.ds(3, 1), pl.ds(1, 4)], in_sem.at[0]),
        pltpu.make_async_copy(gas_hbm.at[pl.ds(0, 3)], g0.at[pl.ds(0, 3), pl.ds(1, 4)], in_sem.at[1]),
        pltpu.make_async_copy(gas_hbm.at[pl.ds(4, 1)], g0.at[pl.ds(4, 1), pl.ds(1, 4)], in_sem.at[2]),
        pltpu.make_async_copy(cell_hbm, cell, in_sem.at[3]),
        pltpu.make_async_copy(state_hbm, state, in_sem.at[4]),
        pltpu.make_async_copy(slot_hbm, slot, in_sem.at[5]),
        pltpu.make_async_copy(dest_hbm, dest, in_sem.at[6]),
    ]
    barrier = pltpu.get_barrier_semaphore()
    for to in (below, above, left, right):
        pl.semaphore_signal(barrier, inc=1, device_id=to, device_id_type=pl.DeviceIdType.MESH)
    for load in loads:
        load.start()
    loads[0].wait()
    stage(0, 3)
    pl.semaphore_wait(barrier, 4)
    send(0, 0)
    loads[1].wait()
    for f in range(3):
        stage(0, f)
    send(0, 1)
    loads[2].wait()
    stage(0, 4)
    acc[...] = jnp.zeros_like(acc)
    rel[...] = jnp.zeros_like(rel)
    receive(0, 0)

    def first_heat(i, carry):
        g1[3, i] = plane(g0, hy0, 3, i)
        return carry
    lax.fori_loop(1, 5, first_heat, 0)
    stage(1, 3)
    send(1, 0)
    send(0, 2)

    receive(0, 1)

    def first_wind(n, carry):
        f, i = n // 4, n % 4 + 1
        fresh = plane(g0, hy0, f, i)
        g1[f, i] = fresh + jnp.where(f == 2, 0.1, 0.0) * g0[3, i]
        return carry
    lax.fori_loop(0, 12, first_wind, 0)
    for f in range(3):
        stage(1, f)
    send(1, 1)
    receive(1, 0)

    def second_heat(i, carry):
        t2[i - 1] = plane(g1, hy1, 3, i)
        return carry
    lax.fori_loop(1, 5, second_heat, 0)
    table(t2[...].reshape(128, 512), tab)
    loads[3].wait()
    steps = 128 // ROWS

    def gather(b, carry):
        gather_block(b, ROWS, cell, tab, seen)
        return carry
    lax.fori_loop(0, steps, gather, 0)
    loads[4].wait()
    burn_all(state, seen[...], state_out, rec)

    receive(0, 2)

    def first_fuel(i, carry):
        g1[4, i] = plane(g0, hy0, 4, i)
        return carry
    lax.fori_loop(1, 5, first_fuel, 0)
    stage(1, 4)
    send(1, 2)

    loads[5].wait()
    loads[6].wait()

    def compact(b, carry):
        compact_block(b, ROWS, slot, dest, rec, acc)
        return carry
    lax.fori_loop(0, steps, compact, 0)
    place = lax.broadcasted_iota(jnp.int32, (8, 256), 0) * 256 + lax.broadcasted_iota(jnp.int32, (8, 256), 1)
    for f in range(4):
        first, second = acc[32 * f:32 * f + 16, :], acc[32 * f + 16:32 * f + 32, :]
        both = first * 256.0 + second if f == 3 else first + second
        for face in range(2):
            live = place < counts_ref[0, face]
            box[face, f] = jnp.where(live, both[8 * face:8 * face + 8], 0.0)
    faces = [
        remote(box.at[0], got.at[1], fs.at[0], fr.at[0], below),
        remote(box.at[1], got.at[0], fs.at[1], fr.at[1], above),
    ]
    for copy in faces:
        copy.start()

    def deposit(b, carry):
        ds = pl.ds(pl.multiple_of(b * ROWS, 8), ROWS)
        burned = jnp.where(slot[ds, :] < 0, rec[2, ds, :], 0.0)
        deposit_block(dest[ds, :], burned, ROWS, rel)
        return carry
    lax.fori_loop(0, steps, deposit, 0)

    receive(1, 1)

    def second_wind(n, carry):
        f, i = n // 4, n % 4 + 1
        fresh = plane(g1, hy1, f, i)
        gas_out[f, i - 1] = fresh + jnp.where(f == 2, 0.1, 0.0) * g1[3, i]
        return carry
    lax.fori_loop(0, 12, second_wind, 0)
    receive(1, 2)

    def second_fuel(i, carry):
        gas_out[4, i - 1] = plane(g1, hy1, 4, i)
        return carry
    lax.fori_loop(1, 5, second_fuel, 0)

    for copy in faces:
        copy.wait_recv()

    @pl.when(p == 0)
    def _():
        got[0] = jnp.zeros((4, 8, 256), F32)

    @pl.when(p == np_ - 1)
    def _():
        got[1] = jnp.zeros((4, 8, 256), F32)

    for d in range(2):
        where_to = got[d, 3].astype(jnp.int32)
        burned = got[d, 2]
        deposit_block(
            jnp.concatenate([where_to[:, :128], where_to[:, 128:]], axis=0),
            jnp.concatenate([burned[:, :128], burned[:, 128:]], axis=0), 16, rel)
        for f in range(3):
            arr_out[f, pl.ds(d, 8, stride=4), :] = got[d, f, :, 0:128]
            arr_out[f, pl.ds(2 + d, 8, stride=4), :] = got[d, f, :, 128:256]
    both = rel[:256, :] + rel[256:, :]
    release = jnp.concatenate([both[:128], both[128:]], axis=1).reshape(4, 32, 512)
    gas_out[3] = t2[...] + 1.5 * release
    gas_out[4] = gas_out[4] + release
    for r in range(2):
        for k in range(3):
            for copy in halo(r, k):
                copy.wait_send()
    for copy in faces:
        copy.wait_send()


def on_device(gas, parcel_state, parcel_cell, parcel_dest, send_slot, face_counts):
    square = lambda a: a.reshape(128, 128)
    state = parcel_state.reshape(2, 128, 128).transpose(1, 0, 2).reshape(256, 128)
    vm = pl.BlockSpec(memory_space=pltpu.VMEM)
    hbm = pl.BlockSpec(memory_space=pltpu.HBM)
    i32 = lambda *s: pltpu.VMEM(s, jnp.int32)
    f32 = lambda *s: pltpu.VMEM(s, F32)
    dma = pltpu.SemaphoreType.DMA
    gas_out, out, arr = pl.pallas_call(
        step_kernel,
        out_shape=(
            jax.ShapeDtypeStruct(gas.shape, F32),
            jax.ShapeDtypeStruct((256, 128), F32),
            jax.ShapeDtypeStruct((3, 32, 128), F32),
        ),
        in_specs=[hbm] * 5 + [pl.BlockSpec(memory_space=pltpu.SMEM)],
        out_specs=(vm, vm, vm),
        scratch_shapes=[
            f32(5, 6, 32, 512), f32(5, 6, 32, 512), f32(4, 32, 512),
            f32(5, 2, 4, 512), f32(5, 2, 4, 512), f32(5, 2, 4, 512), f32(5, 2, 4, 512),
            i32(128, 128), i32(128, 128), i32(128, 128), f32(256, 128),
            pltpu.VMEM((256, 512), BF), f32(128, 128), f32(3, 128, 128), f32(128, 256), f32(512, 256),
            f32(2, 4, 8, 256), f32(2, 4, 8, 256),
            dma((7,)), dma((2, 3, 2)), dma((2, 3, 2)), dma((2, 3, 2)), dma((2, 3, 2)), dma((2,)), dma((2,)),
        ],
        compiler_params=pltpu.CompilerParams(vmem_limit_bytes=60 << 20, collective_id=0, has_side_effects=True),
        name="dust_step",
    )(gas, square(parcel_cell), square(parcel_dest), square(send_slot), state, face_counts.reshape(1, 2))
    parcels_out = out.reshape(128, 2, 128).transpose(1, 0, 2).reshape(2, 16384)
    arrivals = arr.reshape(3, 16, 2, 128).transpose(2, 0, 1, 3).reshape(2, 3, 2048)
    return (gas_out, parcels_out, arrivals)


def solution(mesh):
    in_specs = (
        P(None, "prop", "cross", None),
        P(None, ("prop", "cross")),
        P(("prop", "cross")),
        P(("prop", "cross")),
        P(("prop", "cross")),
        P("prop", "cross", None),
    )
    out_specs = (
        P(None, "prop", "cross", None),
        P(None, ("prop", "cross")),
        P(None, None, ("prop", "cross")),
    )
    return jax.shard_map(
        on_device, mesh=mesh, in_specs=in_specs, out_specs=out_specs, check_vma=False
    )
```

```python
import functools
import jax
import jax.numpy as jnp
from jax import lax
from jax.experimental import pallas as pl
from jax.experimental.pallas import tpu as pltpu
from jax.sharding import PartitionSpec as P

F32 = jnp.float32
BF = jnp.bfloat16
ROWS = 64
NT = (((1,), (1,)), ((), ()))
GROUPS = ((3, 4), (0, 3), (4, 5))


def iota_bf(n):
    return lax.broadcasted_iota(jnp.int32, (n, 128), 0).astype(F32).astype(BF)


def wide(row, n):
    t = jnp.broadcast_to(row, (16, 128)).astype(BF)
    return jnp.concatenate([t] * (n // 16), axis=0)


def split(x):
    hi = x.astype(BF).astype(F32)
    return hi, x - hi


def key_of(cell):
    return (((cell >> 8) & 1) * 128 + (cell >> 9)).astype(F32)


def low_of(cell):
    return (cell & 255).astype(F32)


def half_key(cell, half):
    key = ((cell >> 8) & 1) * 64 + ((cell >> 9) & 63)
    return jnp.where((cell >> 15) == half, key, -1).astype(F32)


def table(T, tab_ref):
    hi, lo = split(T)
    m = jnp.concatenate([hi[:, :256], hi[:, 256:], lo[:, :256], lo[:, 256:]], axis=0)
    tab_ref[...] = m.T.astype(BF)


def gather_block(cell, half, tab_ref):
    rows = cell.shape[0]
    key = half_key(cell, half)
    lo = low_of(cell)
    it = iota_bf(128)
    one = jnp.ones((128, 128), BF)
    zero = jnp.zeros((128, 128), BF)
    oh = jnp.concatenate([jnp.where(it == wide(key[i:i + 1], 128), one, zero) for i in range(rows)], axis=1)
    res = jnp.dot(tab_ref[...], jnp.concatenate([oh, oh], axis=0), preferred_element_type=F32)
    itf = lax.broadcasted_iota(jnp.int32, (256, 128), 0).astype(F32)
    out = []
    for i in range(rows):
        r = res[:, i * 128:(i + 1) * 128]
        out.append(jnp.sum(jnp.where(itf == lo[i:i + 1], r, 0.0), axis=0, keepdims=True))
    return jnp.concatenate(out, axis=0)


def burn_all(state_ref, seen, out_ref, rec_ref):
    mass = state_ref[pl.ds(0, 128, stride=2), :]
    temper = state_ref[pl.ds(1, 128, stride=2), :]
    hot = temper + 0.3 * (seen - temper)
    burned = 0.2 * mass * (1.0 + 0.5 * jnp.tanh(hot))
    left = mass - burned
    warm = hot + 0.5 * burned
    out_ref[pl.ds(0, 128, stride=2), :] = left
    out_ref[pl.ds(1, 128, stride=2), :] = warm
    rec_ref[0] = left
    rec_ref[1] = warm
    rec_ref[2] = burned


def compact_block(b, rows, slot_ref, dest_ref, rec_ref, acc_ref):
    ds = pl.ds(pl.multiple_of(b * rows, 8), rows)
    slot = slot_ref[ds, :]
    dest = dest_ref[ds, :]
    hi = (slot >> 8).astype(F32)
    lo = (slot & 255).astype(F32)
    vals = []
    for f in range(3):
        vals += list(split(rec_ref[f, ds, :]))
    vals += [(dest >> 8).astype(F32), (dest & 255).astype(F32)]
    it = iota_bf(256)
    it16 = iota_bf(16)
    one = jnp.ones((256, 128), BF)
    zero = jnp.zeros((256, 128), BF)
    z16 = jnp.zeros((16, 128), BF)
    As, Bs = [], []
    for i in range(rows):
        Bs.append(jnp.where(it == wide(lo[i:i + 1], 256), one, zero))
        m = it16 == wide(hi[i:i + 1], 16)
        As.append(jnp.concatenate([jnp.where(m, wide(v[i:i + 1], 16), z16) for v in vals], axis=0))
    A = jnp.concatenate(As, axis=1)
    B = jnp.concatenate(Bs, axis=1)
    acc_ref[...] += lax.dot_general(B, A, NT, preferred_element_type=F32)


def deposit_block(dest, burned, rows, acc_ref):
    hi = key_of(dest)
    lo = low_of(dest)
    bh, bl = split(burned)
    it = iota_bf(256)
    one = jnp.ones((256, 128), BF)
    zero = jnp.zeros((256, 128), BF)
    As, Bs = [], []
    for i in range(rows):
        Bs.append(jnp.where(it == wide(lo[i:i + 1], 256), one, zero))
        m = it == wide(hi[i:i + 1], 256)
        As.append(jnp.concatenate([jnp.where(m, wide(bh[i:i + 1], 256), zero), jnp.where(m, wide(bl[i:i + 1], 256), zero)], axis=0))
    A = jnp.concatenate(As, axis=1)
    B = jnp.concatenate(Bs, axis=1)
    acc_ref[...] += lax.dot_general(A, B, NT, preferred_element_type=F32)


def plane(g, hy, f, i):
    c = g[f, i]
    rows, depth = c.shape
    row = lax.broadcasted_iota(jnp.int32, (rows, depth), 0)
    lane = lax.broadcasted_iota(jnp.int32, (rows, depth), 1)
    xm, xp = g[f, i - 1], g[f, i + 1]
    ym = jnp.where(row == 0, hy[f, 0, pl.ds(i - 1, 1), :], pltpu.roll(c, 1, 0))
    yp = jnp.where(row == rows - 1, hy[f, 1, pl.ds(i - 1, 1), :], pltpu.roll(c, rows - 1, 0))
    zm = jnp.where(lane == 0, 0.0, pltpu.roll(c, 1, 1))
    zp = jnp.where(lane == depth - 1, 0.0, pltpu.roll(c, depth - 1, 1))
    advect = g[0, i] * (xp - xm) + g[1, i] * (yp - ym) + g[2, i] * (zp - zm)
    laplace = (xp + xm) + (yp + ym) + (zp + zm) - 6.0 * c
    return c - 0.05 * advect + 0.12 * laplace


def step_kernel(gas_hbm, cell_hbm, dest_hbm, slot_hbm, state_hbm, counts_hbm,
                gas_out, state_out, arr_out,
                g0, g1, t2, hy0, hy1, sy0, sy1, cell, dest, slot, state, counts,
                tab, seen, rec, acc, rel, box, got,
                in_sem, xs, xr, ys, yr, fs, fr):
    p, c = lax.axis_index("prop"), lax.axis_index("cross")
    np_, nc = lax.axis_size("prop"), lax.axis_size("cross")
    side = lax.rem(p, 2)
    below = {"prop": lax.rem(p + np_ - 1, np_)}
    above = {"prop": lax.rem(p + 1, np_)}
    near = {"prop": p + 1 - 2 * side}
    far = {"prop": lax.rem(p + np_ - 1 + 2 * side, np_)}
    left = {"cross": lax.rem(c + nc - 1, nc)}
    right = {"cross": lax.rem(c + 1, nc)}
    near_half, far_half = 1 - side, side
    edge = jnp.logical_or(p == 0, p == np_ - 1)
    gs, hys, sys_ = (g0, g1), (hy0, hy1), (sy0, sy1)

    def remote(a, b, s, r, to):
        return pltpu.make_async_remote_copy(src_ref=a, dst_ref=b, send_sem=s, recv_sem=r, device_id=to, device_id_type=pl.DeviceIdType.MESH)

    def halo_x(r, k, to_far):
        lo, hi = GROUPS[k]
        fields = pl.ds(lo, hi - lo)
        source = 1 + 3 * side if to_far else 4 - 3 * side
        first = gas_hbm.at[fields, source - 1] if r == 0 else g1.at[fields, source]
        goal = 5 * (1 - side) if to_far else 5 * side
        return remote(first, gs[r].at[fields, goal], xs.at[r, k, to_far], xr.at[r, k, to_far], far if to_far else near)

    def halo_y(r, k):
        lo, hi = GROUPS[k]
        fields = pl.ds(lo, hi - lo)
        sy, hy = sys_[r], hys[r]
        return (
            remote(sy.at[fields, 0], hy.at[fields, 1], ys.at[r, k, 0], yr.at[r, k, 0], left),
            remote(sy.at[fields, 1], hy.at[fields, 0], ys.at[r, k, 1], yr.at[r, k, 1], right),
        )

    def stage(r, f):
        for i in range(4):
            sys_[r][f, 0, i:i + 1, :] = gs[r][f, 1 + i, 0:1, :]
            sys_[r][f, 1, i:i + 1, :] = gs[r][f, 1 + i, 31:32, :]

    def send(copies):
        for copy in copies:
            copy.start()

    def receive_near(r, k):
        halo_x(r, k, 0).wait_recv()
        for copy in halo_y(r, k):
            copy.wait_recv()
        lo, hi = GROUPS[k]

        @pl.when(c == 0)
        def _():
            for f in range(lo, hi):
                hys[r][f, 0] = jnp.zeros((4, 512), F32)

        @pl.when(c == nc - 1)
        def _():
            for f in range(lo, hi):
                hys[r][f, 1] = jnp.zeros((4, 512), F32)

    def receive_far(r, k):
        halo_x(r, k, 1).wait_recv()
        lo, hi = GROUPS[k]

        @pl.when(edge)
        def _():
            for f in range(lo, hi):
                gs[r][f, 5 * side] = jnp.zeros((32, 512), F32)

    loads = [
        pltpu.make_async_copy(gas_hbm.at[pl.ds(3, 1)], g0.at[pl.ds(3, 1), pl.ds(1, 4)], in_sem.at[0]),
        pltpu.make_async_copy(gas_hbm.at[pl.ds(0, 3)], g0.at[pl.ds(0, 3), pl.ds(1, 4)], in_sem.at[1]),
        pltpu.make_async_copy(gas_hbm.at[pl.ds(4, 1)], g0.at[pl.ds(4, 1), pl.ds(1, 4)], in_sem.at[2]),
        pltpu.make_async_copy(cell_hbm, cell, in_sem.at[3]),
        pltpu.make_async_copy(state_hbm, state, in_sem.at[4]),
        pltpu.make_async_copy(slot_hbm, slot, in_sem.at[5]),
        pltpu.make_async_copy(dest_hbm, dest, in_sem.at[6]),
        pltpu.make_async_copy(counts_hbm, counts, in_sem.at[7]),
    ]
    barrier = pltpu.get_barrier_semaphore()
    for to in (near, far, left, right):
        pl.semaphore_signal(barrier, inc=1, device_id=to, device_id_type=pl.DeviceIdType.MESH)
    send(loads)
    loads[0].wait()
    stage(0, 3)
    pl.semaphore_wait(barrier, 4)
    send([halo_x(0, 0, 1), halo_x(0, 0, 0)])
    send(halo_y(0, 0))
    send([halo_x(0, 1, 1), halo_x(0, 1, 0)])
    loads[1].wait()
    for f in range(3):
        stage(0, f)
    send(halo_y(0, 1))
    loads[2].wait()
    stage(0, 4)
    send(halo_y(0, 2))
    acc[...] = jnp.zeros_like(acc)
    rel[...] = jnp.zeros_like(rel)
    receive_near(0, 0)
    receive_far(0, 0)

    def first_heat(i, carry):
        g1[3, i] = plane(g0, hy0, 3, i)
        return carry
    lax.fori_loop(1, 5, first_heat, 0)
    send([halo_x(1, 0, 1), halo_x(1, 0, 0)])
    stage(1, 3)
    send(halo_y(1, 0))
    send([halo_x(0, 2, 1), halo_x(0, 2, 0)])

    def first_wind(half):
        def body(n, carry):
            f, i = n // 2, n % 2 + 1 + 2 * half
            fresh = plane(g0, hy0, f, i)
            g1[f, i] = fresh + jnp.where(f == 2, 0.1, 0.0) * g0[3, i]
            return carry
        lax.fori_loop(0, 6, body, 0)

    def first_fuel(half):
        def body(n, carry):
            i = n + 1 + 2 * half
            g1[4, i] = plane(g0, hy0, 4, i)
            return carry
        lax.fori_loop(0, 2, body, 0)

    def second_heat(half):
        def body(n, carry):
            i = n + 2 * half
            t2[i] = plane(g1, hy1, 3, i + 1)
            return carry
        lax.fori_loop(0, 2, body, 0)
        table(t2[pl.ds(2 * half, 2)].reshape(64, 512), tab)

    receive_near(0, 1)
    first_wind(near_half)
    receive_near(0, 2)
    first_fuel(near_half)
    for load in loads[3:]:
        load.wait()
    receive_near(1, 0)
    second_heat(near_half)
    steps = 128 // ROWS

    def near_gather(b, carry):
        ds = pl.ds(pl.multiple_of(b * ROWS, 8), ROWS)
        seen[ds, :] = gather_block(cell[ds, :], near_half, tab)
        return carry
    lax.fori_loop(0, steps, near_gather, 0)

    receive_far(0, 1)
    first_wind(far_half)
    send([halo_x(1, 1, 1), halo_x(1, 1, 0)])
    for f in range(3):
        stage(1, f)
    send(halo_y(1, 1))
    receive_far(1, 0)
    second_heat(far_half)

    def far_gather(b, carry):
        ds = pl.ds(pl.multiple_of(b * ROWS, 8), ROWS)
        seen[ds, :] += gather_block(cell[ds, :], far_half, tab)
        return carry
    lax.fori_loop(0, steps, far_gather, 0)
    burn_all(state, seen[...], state_out, rec)

    receive_far(0, 2)
    first_fuel(far_half)
    send([halo_x(1, 2, 1), halo_x(1, 2, 0)])
    stage(1, 4)
    send(halo_y(1, 2))

    def compact(b, carry):
        compact_block(b, ROWS, slot, dest, rec, acc)
        return carry
    lax.fori_loop(0, steps, compact, 0)
    place = lax.broadcasted_iota(jnp.int32, (8, 256), 0) * 256 + lax.broadcasted_iota(jnp.int32, (8, 256), 1)
    turned = acc[...].T
    for f in range(4):
        first, second = turned[32 * f:32 * f + 16, :], turned[32 * f + 16:32 * f + 32, :]
        both = first * 256.0 + second if f == 3 else first + second
        for face in range(2):
            live = place < counts[0, face]
            box[face, f] = jnp.where(live, both[8 * face:8 * face + 8], 0.0)
    faces = [
        remote(box.at[0], got.at[1], fs.at[0], fr.at[0], below),
        remote(box.at[1], got.at[0], fs.at[1], fr.at[1], above),
    ]
    send(faces)

    def deposit(b, carry):
        ds = pl.ds(pl.multiple_of(b * ROWS, 8), ROWS)
        burned = jnp.where(slot[ds, :] < 0, rec[2, ds, :], 0.0)
        deposit_block(dest[ds, :], burned, ROWS, rel)
        return carry
    lax.fori_loop(0, steps, deposit, 0)

    receive_near(1, 1)
    receive_far(1, 1)

    def second_wind(n, carry):
        f, i = n // 4, n % 4 + 1
        fresh = plane(g1, hy1, f, i)
        gas_out[f, i - 1] = fresh + jnp.where(f == 2, 0.1, 0.0) * g1[3, i]
        return carry
    lax.fori_loop(0, 12, second_wind, 0)
    receive_near(1, 2)
    receive_far(1, 2)

    def second_fuel(i, carry):
        gas_out[4, i - 1] = plane(g1, hy1, 4, i)
        return carry
    lax.fori_loop(1, 5, second_fuel, 0)

    for copy in faces:
        copy.wait_recv()

    @pl.when(p == 0)
    def _():
        got[0] = jnp.zeros((4, 8, 256), F32)

    @pl.when(p == np_ - 1)
    def _():
        got[1] = jnp.zeros((4, 8, 256), F32)

    where_to, burned = [], []
    for d in range(2):
        for part in range(2):
            lanes = slice(128 * part, 128 * part + 128)
            where_to.append(got[d, 3, :, lanes].astype(jnp.int32))
            burned.append(got[d, 2, :, lanes])
            for f in range(3):
                arr_out[f, pl.ds(2 * part + d, 8, stride=4), :] = got[d, f, :, lanes]
    deposit_block(jnp.concatenate(where_to, axis=0), jnp.concatenate(burned, axis=0), 32, rel)
    both = rel[:256, :] + rel[256:, :]
    release = jnp.concatenate([both[:128], both[128:]], axis=1).reshape(4, 32, 512)
    gas_out[3] = t2[...] + 1.5 * release
    gas_out[4] = gas_out[4] + release
    for r in range(2):
        for k in range(3):
            for copy in (halo_x(r, k, 0), halo_x(r, k, 1)) + halo_y(r, k):
                copy.wait_send()
    for copy in faces:
        copy.wait_send()


def on_device(gas, parcel_state, parcel_cell, parcel_dest, send_slot, face_counts):
    square = lambda a: a.reshape(128, 128)
    state = parcel_state.reshape(2, 128, 128).transpose(1, 0, 2).reshape(256, 128)
    vm = pl.BlockSpec(memory_space=pltpu.VMEM)
    hbm = pl.BlockSpec(memory_space=pltpu.HBM)
    i32 = lambda *s: pltpu.VMEM(s, jnp.int32)
    f32 = lambda *s: pltpu.VMEM(s, F32)
    dma = pltpu.SemaphoreType.DMA
    inputs = (gas, square(parcel_cell), square(parcel_dest), square(send_slot), state, face_counts.reshape(1, 2))
    gas_out, out, arr = pl.pallas_call(
        step_kernel,
        out_shape=(
            jax.ShapeDtypeStruct(gas.shape, F32),
            jax.ShapeDtypeStruct((256, 128), F32),
            jax.ShapeDtypeStruct((3, 32, 128), F32),
        ),
        in_specs=[hbm] * 6,
        out_specs=(vm, vm, vm),
        scratch_shapes=[
            f32(5, 6, 32, 512), f32(5, 6, 32, 512), f32(4, 32, 512),
            f32(5, 2, 4, 512), f32(5, 2, 4, 512), f32(5, 2, 4, 512), f32(5, 2, 4, 512),
            i32(128, 128), i32(128, 128), i32(128, 128), f32(256, 128), pltpu.SMEM((1, 2), jnp.int32),
            pltpu.VMEM((256, 256), BF), f32(128, 128), f32(3, 128, 128), f32(256, 128), f32(512, 256),
            f32(2, 4, 8, 256), f32(2, 4, 8, 256),
            dma((8,)), dma((2, 3, 2)), dma((2, 3, 2)), dma((2, 3, 2)), dma((2, 3, 2)), dma((2,)), dma((2,)),
        ],
        compiler_params=pltpu.CompilerParams(vmem_limit_bytes=44 << 20, collective_id=0, has_side_effects=True),
        name="dust_step",
    )(*[pltpu.with_memory_space_constraint(a, pltpu.HBM) for a in inputs])
    parcels_out = out.reshape(128, 2, 128).transpose(1, 0, 2).reshape(2, 16384)
    arrivals = arr.reshape(3, 16, 2, 128).transpose(2, 0, 1, 3).reshape(2, 3, 2048)
    return (gas_out, parcels_out, arrivals)


def solution(mesh):
    in_specs = (
        P(None, "prop", "cross", None),
        P(None, ("prop", "cross")),
        P(("prop", "cross")),
        P(("prop", "cross")),
        P(("prop", "cross")),
        P("prop", "cross", None),
    )
    out_specs = (
        P(None, "prop", "cross", None),
        P(None, ("prop", "cross")),
        P(None, None, ("prop", "cross")),
    )
    return jax.shard_map(
        on_device, mesh=mesh, in_specs=in_specs, out_specs=out_specs, check_vma=False
    )
```

```python
import functools
import jax
import jax.numpy as jnp
from jax import lax
from jax.experimental import pallas as pl
from jax.experimental.pallas import tpu as pltpu
from jax.sharding import PartitionSpec as P

F32 = jnp.float32
BF = jnp.bfloat16
ROWS = 64
NT = (((1,), (1,)), ((), ()))
GROUPS = ((3, 4), (0, 3), (4, 5))


def iota_bf(n):
    return lax.broadcasted_iota(jnp.int32, (n, 128), 0).astype(F32).astype(BF)


def wide(row, n):
    t = jnp.broadcast_to(row, (16, 128)).astype(BF)
    return jnp.concatenate([t] * (n // 16), axis=0)


def split(x):
    hi = x.astype(BF).astype(F32)
    return hi, x - hi


def key_of(cell):
    return (((cell >> 8) & 1) * 128 + (cell >> 9)).astype(F32)


def low_of(cell):
    return (cell & 255).astype(F32)


def half_key(cell, half):
    key = ((cell >> 8) & 1) * 64 + ((cell >> 9) & 63)
    return jnp.where((cell >> 15) == half, key, -1).astype(F32)


def table(T, tab_ref):
    hi, lo = split(T)
    m = jnp.concatenate([hi[:, :256], hi[:, 256:], lo[:, :256], lo[:, 256:]], axis=0)
    tab_ref[...] = m.T.astype(BF)


def gather_block(cell, half, tab_ref):
    rows = cell.shape[0]
    key = half_key(cell, half)
    lo = low_of(cell)
    it = iota_bf(128)
    one = jnp.ones((128, 128), BF)
    zero = jnp.zeros((128, 128), BF)
    oh = jnp.concatenate([jnp.where(it == wide(key[i:i + 1], 128), one, zero) for i in range(rows)], axis=1)
    res = jnp.dot(tab_ref[...], jnp.concatenate([oh, oh], axis=0), preferred_element_type=F32)
    itf = lax.broadcasted_iota(jnp.int32, (256, 128), 0).astype(F32)
    out = []
    for i in range(rows):
        r = res[:, i * 128:(i + 1) * 128]
        out.append(jnp.sum(jnp.where(itf == lo[i:i + 1], r, 0.0), axis=0, keepdims=True))
    return jnp.concatenate(out, axis=0)


def burn_all(state_ref, seen, out_ref, rec_ref):
    mass = state_ref[pl.ds(0, 128, stride=2), :]
    temper = state_ref[pl.ds(1, 128, stride=2), :]
    hot = temper + 0.3 * (seen - temper)
    burned = 0.2 * mass * (1.0 + 0.5 * jnp.tanh(hot))
    left = mass - burned
    warm = hot + 0.5 * burned
    out_ref[pl.ds(0, 128, stride=2), :] = left
    out_ref[pl.ds(1, 128, stride=2), :] = warm
    rec_ref[0] = left
    rec_ref[1] = warm
    rec_ref[2] = burned


def compact_block(b, rows, slot_ref, dest_ref, rec_ref, acc_ref):
    ds = pl.ds(pl.multiple_of(b * rows, 8), rows)
    slot = slot_ref[ds, :]
    dest = dest_ref[ds, :]
    hi = (slot >> 8).astype(F32)
    lo = (slot & 255).astype(F32)
    vals = []
    for f in range(3):
        vals += list(split(rec_ref[f, ds, :]))
    vals += [(dest >> 8).astype(F32), (dest & 255).astype(F32)]
    it = iota_bf(256)
    it16 = iota_bf(16)
    one = jnp.ones((256, 128), BF)
    zero = jnp.zeros((256, 128), BF)
    z16 = jnp.zeros((16, 128), BF)
    As, Bs = [], []
    for i in range(rows):
        Bs.append(jnp.where(it == wide(lo[i:i + 1], 256), one, zero))
        m = it16 == wide(hi[i:i + 1], 16)
        As.append(jnp.concatenate([jnp.where(m, wide(v[i:i + 1], 16), z16) for v in vals], axis=0))
    A = jnp.concatenate(As, axis=1)
    B = jnp.concatenate(Bs, axis=1)
    acc_ref[...] += lax.dot_general(B, A, NT, preferred_element_type=F32)


def deposit_block(dest, burned, rows, acc_ref):
    hi = key_of(dest)
    lo = low_of(dest)
    bh, bl = split(burned)
    it = iota_bf(256)
    one = jnp.ones((256, 128), BF)
    zero = jnp.zeros((256, 128), BF)
    As, Bs = [], []
    for i in range(rows):
        Bs.append(jnp.where(it == wide(lo[i:i + 1], 256), one, zero))
        m = it == wide(hi[i:i + 1], 256)
        As.append(jnp.concatenate([jnp.where(m, wide(bh[i:i + 1], 256), zero), jnp.where(m, wide(bl[i:i + 1], 256), zero)], axis=0))
    A = jnp.concatenate(As, axis=1)
    B = jnp.concatenate(Bs, axis=1)
    acc_ref[...] += lax.dot_general(A, B, NT, preferred_element_type=F32)


def plane(g, hy, f, i):
    c = g[f, i]
    rows, depth = c.shape
    row = lax.broadcasted_iota(jnp.int32, (8, depth), 0)
    lane = lax.broadcasted_iota(jnp.int32, (rows, 128), 1)
    xm, xp = g[f, i - 1], g[f, i + 1]
    down, up = pltpu.roll(c, 1, 0), pltpu.roll(c, rows - 1, 0)
    ym = jnp.concatenate([jnp.where(row == 0, hy[f, 0, pl.ds(i - 1, 1), :], down[:8]), down[8:]], axis=0)
    yp = jnp.concatenate([up[:-8], jnp.where(row == 7, hy[f, 1, pl.ds(i - 1, 1), :], up[-8:])], axis=0)
    back, on = pltpu.roll(c, 1, 1), pltpu.roll(c, depth - 1, 1)
    zm = jnp.concatenate([jnp.where(lane == 0, 0.0, back[:, :128]), back[:, 128:]], axis=1)
    zp = jnp.concatenate([on[:, :-128], jnp.where(lane == 127, 0.0, on[:, -128:])], axis=1)
    advect = g[0, i] * (xp - xm) + g[1, i] * (yp - ym) + g[2, i] * (zp - zm)
    around = (xp + xm) + (yp + ym) + (zp + zm)
    return (0.28 * c + 0.12 * around) - 0.05 * advect


def step_kernel(gas_hbm, cell_hbm, dest_hbm, slot_hbm, state_hbm, counts_hbm,
                gas_out, state_out, arr_out,
                g0, g1, t2, hy0, hy1, sy0, sy1, cell, dest, slot, state, counts,
                tab, seen, rec, acc, rel, box, got,
                in_sem, fars, farr, xs, xr, ys, yr, fs, fr):
    p, c = lax.axis_index("prop"), lax.axis_index("cross")
    np_, nc = lax.axis_size("prop"), lax.axis_size("cross")
    side = lax.rem(p, 2)
    below = {"prop": lax.rem(p + np_ - 1, np_)}
    above = {"prop": lax.rem(p + 1, np_)}
    near = {"prop": p + 1 - 2 * side}
    far = {"prop": lax.rem(p + np_ - 1 + 2 * side, np_)}
    left = {"cross": lax.rem(c + nc - 1, nc)}
    right = {"cross": lax.rem(c + 1, nc)}
    near_half, far_half = 1 - side, side
    inner, outer, rest = 4 - 3 * side, 1 + 3 * side, 2 - side
    has_below, has_above, has_left, has_right = p > 0, p < np_ - 1, c > 0, c < nc - 1
    edge = jnp.logical_or(p == 0, p == np_ - 1)
    has_far = jnp.logical_not(edge)
    gs, hys, sys_ = (g0, g1), (hy0, hy1), (sy0, sy1)

    def remote(a, b, s, r, to):
        return pltpu.make_async_remote_copy(src_ref=a, dst_ref=b, send_sem=s, recv_sem=r, device_id=to, device_id_type=pl.DeviceIdType.MESH)

    def halo_far(r, f):
        source = gas_hbm.at[f, outer - 1] if r == 0 else g1.at[f, outer]
        return remote(source, gs[r].at[f, 5 * (1 - side)], fars.at[r, f], farr.at[r, f], far)

    def halo_near(r, k):
        lo, hi = GROUPS[k]
        fields = pl.ds(lo, hi - lo)
        source = gas_hbm.at[fields, inner - 1] if r == 0 else g1.at[fields, inner]
        return remote(source, gs[r].at[fields, 5 * side], xs.at[r, k], xr.at[r, k], near)

    def halo_y(r, k, d):
        lo, hi = GROUPS[k]
        fields = pl.ds(lo, hi - lo)
        return remote(sys_[r].at[fields, d], hys[r].at[fields, 1 - d], ys.at[r, k, d], yr.at[r, k, d], right if d else left)

    def stage(r, k):
        for f in range(*GROUPS[k]):
            for i in range(4):
                sys_[r][f, 0, i:i + 1, :] = gs[r][f, 1 + i, 0:1, :]
                sys_[r][f, 1, i:i + 1, :] = gs[r][f, 1 + i, 31:32, :]

    def send_far(r, *fields):
        @pl.when(has_far)
        def _():
            for f in fields:
                halo_far(r, f).start()

    def send_near(r, k):
        halo_near(r, k).start()

    def send_y(r, *groups):
        @pl.when(has_left)
        def _():
            for k in groups:
                halo_y(r, k, 0).start()

        @pl.when(has_right)
        def _():
            for k in groups:
                halo_y(r, k, 1).start()

    def receive_near(r, k):
        halo_near(r, k).wait_recv()

        @pl.when(has_left)
        def _():
            halo_y(r, k, 1).wait_recv()

        @pl.when(has_right)
        def _():
            halo_y(r, k, 0).wait_recv()

    def receive_far(r, *fields):
        @pl.when(has_far)
        def _():
            for f in fields:
                halo_far(r, f).wait_recv()

    def first(f, i):
        fresh = plane(g0, hy0, f, i)
        g1[f, i] = fresh + 0.1 * g0[3, i] if f == 2 else fresh

    def second(f, i):
        fresh = plane(g1, hy1, f, i)
        gas_out[f, i - 1] = fresh + 0.1 * g1[3, i] if f == 2 else fresh

    def on_rest(todo):
        def body(n, carry):
            todo(rest + n)
            return carry
        lax.fori_loop(0, 3, body, 0)

    loads = [
        pltpu.make_async_copy(gas_hbm.at[pl.ds(3, 1)], g0.at[pl.ds(3, 1), pl.ds(1, 4)], in_sem.at[0]),
        pltpu.make_async_copy(gas_hbm.at[pl.ds(0, 3)], g0.at[pl.ds(0, 3), pl.ds(1, 4)], in_sem.at[1]),
        pltpu.make_async_copy(gas_hbm.at[pl.ds(4, 1)], g0.at[pl.ds(4, 1), pl.ds(1, 4)], in_sem.at[2]),
        pltpu.make_async_copy(cell_hbm, cell, in_sem.at[3]),
        pltpu.make_async_copy(state_hbm, state, in_sem.at[4]),
        pltpu.make_async_copy(slot_hbm, slot, in_sem.at[5]),
        pltpu.make_async_copy(dest_hbm, dest, in_sem.at[6]),
        pltpu.make_async_copy(counts_hbm, counts, in_sem.at[7]),
    ]
    barrier = pltpu.get_barrier_semaphore()
    def greet(to):
        pl.semaphore_signal(barrier, inc=1, device_id=to, device_id_type=pl.DeviceIdType.MESH)

    greet(near)
    pl.when(has_far)(lambda: greet(far))
    pl.when(has_left)(lambda: greet(left))
    pl.when(has_right)(lambda: greet(right))
    for load in loads:
        load.start()

    @pl.when(edge)
    def _():
        for g in gs:
            for f in range(5):
                g[f, 5 * side] = jnp.zeros((32, 512), F32)

    @pl.when(c == 0)
    def _():
        for hy in hys:
            hy[:, 0] = jnp.zeros((5, 4, 512), F32)

    @pl.when(c == nc - 1)
    def _():
        for hy in hys:
            hy[:, 1] = jnp.zeros((5, 4, 512), F32)

    @pl.when(p == 0)
    def _():
        got[0] = jnp.zeros((4, 8, 256), F32)

    @pl.when(p == np_ - 1)
    def _():
        got[1] = jnp.zeros((4, 8, 256), F32)

    loads[0].wait()
    stage(0, 0)
    loads[1].wait()
    stage(0, 1)
    loads[2].wait()
    stage(0, 2)
    pl.semaphore_wait(barrier, 1 + has_far.astype(jnp.int32) + has_left.astype(jnp.int32) + has_right.astype(jnp.int32))
    send_y(0, 0)
    send_far(0, 3)
    send_near(0, 0)
    send_y(0, 1, 2)
    send_far(0, 0, 1)
    send_near(0, 1)
    send_near(0, 2)
    acc[...] = jnp.zeros_like(acc)
    rel[...] = jnp.zeros_like(rel)

    receive_near(0, 0)
    on_rest(lambda i: first(3, i))
    receive_far(0, 3)
    first(3, outer)
    stage(1, 0)
    send_y(1, 0)
    send_near(1, 0)
    send_far(0, 2)
    send_far(1, 3)
    send_far(0, 4)
    receive_near(0, 1)

    def winds(i):
        for f in range(3):
            first(f, i)
    on_rest(winds)
    receive_near(0, 2)
    on_rest(lambda i: first(4, i))
    for load in loads[3:]:
        load.wait()

    def second_heat(half):
        def body(n, carry):
            i = n + 2 * half
            t2[i] = plane(g1, hy1, 3, i + 1)
            return carry
        lax.fori_loop(0, 2, body, 0)
        table(t2[pl.ds(2 * half, 2)].reshape(64, 512), tab)

    def on_blocks(todo):
        def body(b, carry):
            todo(b, pl.ds(pl.multiple_of(b * ROWS, 8), ROWS))
            return carry
        lax.fori_loop(0, 128 // ROWS, body, 0)

    receive_near(1, 0)
    second_heat(near_half)

    def near_gather(b, ds):
        seen[ds, :] = gather_block(cell[ds, :], near_half, tab)
    on_blocks(near_gather)

    receive_far(0, 0, 1, 2)
    winds(outer)
    stage(1, 1)
    send_y(1, 1)
    send_far(1, 0, 1, 2)
    send_near(1, 1)
    receive_far(1, 3)
    second_heat(far_half)

    def far_gather(b, ds):
        seen[ds, :] += gather_block(cell[ds, :], far_half, tab)
    on_blocks(far_gather)
    receive_far(0, 4)
    first(4, outer)
    stage(1, 2)
    send_y(1, 2)
    send_far(1, 4)
    send_near(1, 2)
    burn_all(state, seen[...], state_out, rec)
    on_blocks(lambda b, ds: compact_block(b, ROWS, slot, dest, rec, acc))
    place = lax.broadcasted_iota(jnp.int32, (8, 256), 0) * 256 + lax.broadcasted_iota(jnp.int32, (8, 256), 1)
    turned = acc[...].T
    for f in range(4):
        head, tail = turned[32 * f:32 * f + 16, :], turned[32 * f + 16:32 * f + 32, :]
        both = head * 256.0 + tail if f == 3 else head + tail
        for face in range(2):
            live = place < counts[0, face]
            box[face, f] = jnp.where(live, both[8 * face:8 * face + 8], 0.0)
    down = remote(box.at[0], got.at[1], fs.at[0], fr.at[0], below)
    up = remote(box.at[1], got.at[0], fs.at[1], fr.at[1], above)
    pl.when(has_below)(down.start)
    pl.when(has_above)(up.start)

    def deposit(b, ds):
        burned = jnp.where(slot[ds, :] < 0, rec[2, ds, :], 0.0)
        deposit_block(dest[ds, :], burned, ROWS, rel)
    on_blocks(deposit)

    receive_near(1, 1)

    def later_winds(i):
        for f in range(3):
            second(f, i)
    on_rest(later_winds)
    receive_near(1, 2)
    on_rest(lambda i: second(4, i))
    for f in (0, 1, 2, 4):
        receive_far(1, f)
        second(f, outer)

    pl.when(has_below)(up.wait_recv)
    pl.when(has_above)(down.wait_recv)
    where_to, burned = [], []
    for d in range(2):
        for part in range(2):
            lanes = slice(128 * part, 128 * part + 128)
            where_to.append(got[d, 3, :, lanes].astype(jnp.int32))
            burned.append(got[d, 2, :, lanes])
            for f in range(3):
                arr_out[f, pl.ds(2 * part + d, 8, stride=4), :] = got[d, f, :, lanes]
    deposit_block(jnp.concatenate(where_to, axis=0), jnp.concatenate(burned, axis=0), 32, rel)
    both = rel[:256, :] + rel[256:, :]
    release = jnp.concatenate([both[:128], both[128:]], axis=1).reshape(4, 32, 512)
    gas_out[3] = t2[...] + 1.5 * release
    gas_out[4] = gas_out[4] + release

    @pl.when(has_far)
    def _():
        for r in range(2):
            for f in range(5):
                halo_far(r, f).wait_send()

    for r in range(2):
        for k in range(3):
            halo_near(r, k).wait_send()
    for d, there in ((0, has_left), (1, has_right)):
        @pl.when(there)
        def _():
            for r in range(2):
                for k in range(3):
                    halo_y(r, k, d).wait_send()
    pl.when(has_below)(down.wait_send)
    pl.when(has_above)(up.wait_send)


def on_device(gas, parcel_state, parcel_cell, parcel_dest, send_slot, face_counts):
    square = lambda a: a.reshape(128, 128)
    state = parcel_state.reshape(2, 128, 128).transpose(1, 0, 2).reshape(256, 128)
    vm = pl.BlockSpec(memory_space=pltpu.VMEM)
    hbm = pl.BlockSpec(memory_space=pltpu.HBM)
    i32 = lambda *s: pltpu.VMEM(s, jnp.int32)
    f32 = lambda *s: pltpu.VMEM(s, F32)
    dma = pltpu.SemaphoreType.DMA
    inputs = (gas, square(parcel_cell), square(parcel_dest), square(send_slot), state, face_counts.reshape(1, 2))
    gas_out, out, arr = pl.pallas_call(
        step_kernel,
        out_shape=(
            jax.ShapeDtypeStruct(gas.shape, F32),
            jax.ShapeDtypeStruct((256, 128), F32),
            jax.ShapeDtypeStruct((3, 32, 128), F32),
        ),
        in_specs=[hbm] * 6,
        out_specs=(vm, vm, vm),
        scratch_shapes=[
            f32(5, 6, 32, 512), f32(5, 6, 32, 512), f32(4, 32, 512),
            f32(5, 2, 4, 512), f32(5, 2, 4, 512), f32(5, 2, 4, 512), f32(5, 2, 4, 512),
            i32(128, 128), i32(128, 128), i32(128, 128), f32(256, 128), pltpu.SMEM((1, 2), jnp.int32),
            pltpu.VMEM((256, 256), BF), f32(128, 128), f32(3, 128, 128), f32(256, 128), f32(512, 256),
            f32(2, 4, 8, 256), f32(2, 4, 8, 256),
            dma((8,)), dma((2, 5)), dma((2, 5)), dma((2, 3)), dma((2, 3)), dma((2, 3, 2)), dma((2, 3, 2)), dma((2,)), dma((2,)),
        ],
        compiler_params=pltpu.CompilerParams(vmem_limit_bytes=44 << 20, collective_id=0, has_side_effects=True),
        name="dust_step",
    )(*[pltpu.with_memory_space_constraint(a, pltpu.HBM) for a in inputs])
    parcels_out = out.reshape(128, 2, 128).transpose(1, 0, 2).reshape(2, 16384)
    arrivals = arr.reshape(3, 16, 2, 128).transpose(2, 0, 1, 3).reshape(2, 3, 2048)
    return (gas_out, parcels_out, arrivals)


def solution(mesh):
    in_specs = (
        P(None, "prop", "cross", None),
        P(None, ("prop", "cross")),
        P(("prop", "cross")),
        P(("prop", "cross")),
        P(("prop", "cross")),
        P("prop", "cross", None),
    )
    out_specs = (
        P(None, "prop", "cross", None),
        P(None, ("prop", "cross")),
        P(None, None, ("prop", "cross")),
    )
    return jax.shard_map(
        on_device, mesh=mesh, in_specs=in_specs, out_specs=out_specs, check_vma=False
    )
```

```python
import functools
import jax
import jax.numpy as jnp
from jax import lax
from jax.experimental import pallas as pl
from jax.experimental.pallas import tpu as pltpu
from jax.sharding import PartitionSpec as P

F32 = jnp.float32
BF = jnp.bfloat16
ROWS = 64
NT = (((1,), (1,)), ((), ()))
GROUPS = ((3, 4), (0, 3), (4, 5))


def iota_bf(n):
    return lax.broadcasted_iota(jnp.int32, (n, 128), 0).astype(F32).astype(BF)


def wide(row, n):
    t = jnp.broadcast_to(row, (16, 128)).astype(BF)
    return jnp.concatenate([t] * (n // 16), axis=0)


def split(x):
    hi = x.astype(BF).astype(F32)
    return hi, x - hi


def key_of(cell):
    return (((cell >> 8) & 1) * 128 + (cell >> 9)).astype(F32)


def low_of(cell):
    return (cell & 255).astype(F32)


def half_key(cell, half):
    key = ((cell >> 8) & 1) * 64 + ((cell >> 9) & 63)
    return jnp.where((cell >> 15) == half, key, -1).astype(F32)


def table(T, tab_ref):
    hi, lo = split(T)
    m = jnp.concatenate([hi[:, :256], hi[:, 256:], lo[:, :256], lo[:, 256:]], axis=0)
    tab_ref[...] = m.T.astype(BF)


def gather_block(cell, half, tab_ref):
    rows = cell.shape[0]
    key = half_key(cell, half)
    lo = low_of(cell)
    it = iota_bf(128)
    one = jnp.ones((128, 128), BF)
    zero = jnp.zeros((128, 128), BF)
    oh = jnp.concatenate([jnp.where(it == wide(key[i:i + 1], 128), one, zero) for i in range(rows)], axis=1)
    res = jnp.dot(tab_ref[...], jnp.concatenate([oh, oh], axis=0), preferred_element_type=F32)
    itf = lax.broadcasted_iota(jnp.int32, (256, 128), 0).astype(F32)
    out = []
    for i in range(rows):
        r = res[:, i * 128:(i + 1) * 128]
        out.append(jnp.sum(jnp.where(itf == lo[i:i + 1], r, 0.0), axis=0, keepdims=True))
    return jnp.concatenate(out, axis=0)


def burn(mass, temper, seen):
    hot = temper + 0.3 * (seen - temper)
    burned = 0.2 * mass * (1.0 + 0.5 * jnp.tanh(hot))
    return mass - burned, hot + 0.5 * burned, burned


def compact_block(b, rows, slot, dest, cell, mass, temper, acc_ref):
    hi = (slot >> 8).astype(F32)
    lo = (slot & 255).astype(F32)
    vals = [*split(mass), *split(temper)]
    for index in (cell, dest):
        vals += [(index >> 8).astype(F32), (index & 255).astype(F32)]
    it = iota_bf(256)
    it16 = iota_bf(16)
    one = jnp.ones((256, 128), BF)
    zero = jnp.zeros((256, 128), BF)
    z16 = jnp.zeros((16, 128), BF)
    As, Bs = [], []
    for i in range(rows):
        Bs.append(jnp.where(it == wide(lo[i:i + 1], 256), one, zero))
        m = it16 == wide(hi[i:i + 1], 16)
        As.append(jnp.concatenate([jnp.where(m, wide(v[i:i + 1], 16), z16) for v in vals], axis=0))
    A = jnp.concatenate(As, axis=1)
    B = jnp.concatenate(Bs, axis=1)
    acc_ref[...] += lax.dot_general(B, A, NT, preferred_element_type=F32)


def deposit_block(dest, burned, rows, acc_ref):
    hi = key_of(dest)
    lo = low_of(dest)
    bh, bl = split(burned)
    it = iota_bf(256)
    one = jnp.ones((256, 128), BF)
    zero = jnp.zeros((256, 128), BF)
    As, Bs = [], []
    for i in range(rows):
        Bs.append(jnp.where(it == wide(lo[i:i + 1], 256), one, zero))
        m = it == wide(hi[i:i + 1], 256)
        As.append(jnp.concatenate([jnp.where(m, wide(bh[i:i + 1], 256), zero), jnp.where(m, wide(bl[i:i + 1], 256), zero)], axis=0))
    A = jnp.concatenate(As, axis=1)
    B = jnp.concatenate(Bs, axis=1)
    acc_ref[...] += lax.dot_general(A, B, NT, preferred_element_type=F32)


def plane(g, hy, f, i):
    c = g[f, i]
    rows, depth = c.shape
    row = lax.broadcasted_iota(jnp.int32, (8, depth), 0)
    lane = lax.broadcasted_iota(jnp.int32, (rows, 128), 1)
    xm, xp = g[f, i - 1], g[f, i + 1]
    down, up = pltpu.roll(c, 1, 0), pltpu.roll(c, rows - 1, 0)
    ym = jnp.concatenate([jnp.where(row == 0, hy[f, 0, pl.ds(i - 1, 1), :], down[:8]), down[8:]], axis=0)
    yp = jnp.concatenate([up[:-8], jnp.where(row == 7, hy[f, 1, pl.ds(i - 1, 1), :], up[-8:])], axis=0)
    back, on = pltpu.roll(c, 1, 1), pltpu.roll(c, depth - 1, 1)
    zm = jnp.concatenate([jnp.where(lane == 0, 0.0, back[:, :128]), back[:, 128:]], axis=1)
    zp = jnp.concatenate([on[:, :-128], jnp.where(lane == 127, 0.0, on[:, -128:])], axis=1)
    advect = g[0, i] * (xp - xm) + g[1, i] * (yp - ym) + g[2, i] * (zp - zm)
    around = (xp + xm) + (yp + ym) + (zp + zm)
    return (0.28 * c + 0.12 * around) - 0.05 * advect


def step_kernel(gas_hbm, cell_hbm, dest_hbm, slot_hbm, state_hbm, counts_hbm,
                gas_out, state_out, arr_out,
                g0, g1, t2, hy0, hy1, sy0, sy1, cell, dest, slot, state, counts,
                tab, seen, leaver, stay, acc, rel, box, got,
                in_sem, fars, farr, xs, xr, ys, yr, fs, fr):
    p, c = lax.axis_index("prop"), lax.axis_index("cross")
    np_, nc = lax.axis_size("prop"), lax.axis_size("cross")
    side = lax.rem(p, 2)
    below = {"prop": lax.rem(p + np_ - 1, np_)}
    above = {"prop": lax.rem(p + 1, np_)}
    near = {"prop": p + 1 - 2 * side}
    far = {"prop": lax.rem(p + np_ - 1 + 2 * side, np_)}
    left = {"cross": lax.rem(c + nc - 1, nc)}
    right = {"cross": lax.rem(c + 1, nc)}
    near_half, far_half = 1 - side, side
    inner, outer, rest = 4 - 3 * side, 1 + 3 * side, 2 - side
    has_below, has_above, has_left, has_right = p > 0, p < np_ - 1, c > 0, c < nc - 1
    edge = jnp.logical_or(p == 0, p == np_ - 1)
    has_far = jnp.logical_not(edge)
    gs, hys, sys_ = (g0, g1), (hy0, hy1), (sy0, sy1)

    def remote(a, b, s, r, to):
        return pltpu.make_async_remote_copy(src_ref=a, dst_ref=b, send_sem=s, recv_sem=r, device_id=to, device_id_type=pl.DeviceIdType.MESH)

    def halo_far(r, f):
        source = gas_hbm.at[f, outer - 1] if r == 0 else g1.at[f, outer]
        return remote(source, gs[r].at[f, 5 * (1 - side)], fars.at[r, f], farr.at[r, f], far)

    def halo_near(r, k):
        lo, hi = GROUPS[k]
        fields = pl.ds(lo, hi - lo)
        source = gas_hbm.at[fields, inner - 1] if r == 0 else g1.at[fields, inner]
        return remote(source, gs[r].at[fields, 5 * side], xs.at[r, k], xr.at[r, k], near)

    def halo_y(r, k, d):
        lo, hi = GROUPS[k]
        fields = pl.ds(lo, hi - lo)
        return remote(sys_[r].at[fields, d], hys[r].at[fields, 1 - d], ys.at[r, k, d], yr.at[r, k, d], right if d else left)

    def stage(r, k):
        for f in range(*GROUPS[k]):
            for i in range(4):
                sys_[r][f, 0, i:i + 1, :] = gs[r][f, 1 + i, 0:1, :]
                sys_[r][f, 1, i:i + 1, :] = gs[r][f, 1 + i, 31:32, :]

    def send_far(r, *fields):
        @pl.when(has_far)
        def _():
            for f in fields:
                halo_far(r, f).start()

    def send_near(r, k):
        halo_near(r, k).start()

    def send_y(r, *groups):
        @pl.when(has_left)
        def _():
            for k in groups:
                halo_y(r, k, 0).start()

        @pl.when(has_right)
        def _():
            for k in groups:
                halo_y(r, k, 1).start()

    def receive_near(r, k):
        halo_near(r, k).wait_recv()

        @pl.when(has_left)
        def _():
            halo_y(r, k, 1).wait_recv()

        @pl.when(has_right)
        def _():
            halo_y(r, k, 0).wait_recv()

    def receive_far(r, *fields):
        @pl.when(has_far)
        def _():
            for f in fields:
                halo_far(r, f).wait_recv()

    def first(f, i):
        fresh = plane(g0, hy0, f, i)
        g1[f, i] = fresh + 0.1 * g0[3, i] if f == 2 else fresh

    def second(f, i):
        fresh = plane(g1, hy1, f, i)
        gas_out[f, i - 1] = fresh + 0.1 * g1[3, i] if f == 2 else fresh

    def on_rest(todo):
        def body(n, carry):
            todo(rest + n)
            return carry
        lax.fori_loop(0, 3, body, 0)

    loads = [
        pltpu.make_async_copy(gas_hbm.at[pl.ds(3, 1)], g0.at[pl.ds(3, 1), pl.ds(1, 4)], in_sem.at[0]),
        pltpu.make_async_copy(gas_hbm.at[pl.ds(0, 3)], g0.at[pl.ds(0, 3), pl.ds(1, 4)], in_sem.at[1]),
        pltpu.make_async_copy(gas_hbm.at[pl.ds(4, 1)], g0.at[pl.ds(4, 1), pl.ds(1, 4)], in_sem.at[2]),
        pltpu.make_async_copy(cell_hbm, cell.at[pl.ds(0, 128)], in_sem.at[3]),
        pltpu.make_async_copy(state_hbm, state, in_sem.at[4]),
        pltpu.make_async_copy(slot_hbm, slot, in_sem.at[5]),
        pltpu.make_async_copy(dest_hbm, dest, in_sem.at[6]),
        pltpu.make_async_copy(counts_hbm, counts, in_sem.at[7]),
    ]
    barrier = pltpu.get_barrier_semaphore()
    def greet(to):
        pl.semaphore_signal(barrier, inc=1, device_id=to, device_id_type=pl.DeviceIdType.MESH)

    greet(near)
    pl.when(has_far)(lambda: greet(far))
    pl.when(has_left)(lambda: greet(left))
    pl.when(has_right)(lambda: greet(right))
    for load in loads:
        load.start()

    @pl.when(edge)
    def _():
        for g in gs:
            for f in range(5):
                g[f, 5 * side] = jnp.zeros((32, 512), F32)

    @pl.when(c == 0)
    def _():
        for hy in hys:
            hy[:, 0] = jnp.zeros((5, 4, 512), F32)

    @pl.when(c == nc - 1)
    def _():
        for hy in hys:
            hy[:, 1] = jnp.zeros((5, 4, 512), F32)

    @pl.when(p == 0)
    def _():
        got[0] = jnp.zeros((4, 8, 256), F32)

    @pl.when(p == np_ - 1)
    def _():
        got[1] = jnp.zeros((4, 8, 256), F32)

    loads[0].wait()
    stage(0, 0)
    loads[1].wait()
    stage(0, 1)
    loads[2].wait()
    stage(0, 2)
    pl.semaphore_wait(barrier, 1 + has_far.astype(jnp.int32) + has_left.astype(jnp.int32) + has_right.astype(jnp.int32))
    send_y(0, 0)
    send_far(0, 3)
    send_near(0, 0)
    send_y(0, 1, 2)
    send_far(0, 0, 1)
    send_near(0, 1)
    send_near(0, 2)
    acc[...] = jnp.zeros_like(acc)
    rel[...] = jnp.zeros_like(rel)
    for load in loads[3:]:
        load.wait()

    def on_blocks(rows, todo):
        def body(b, carry):
            todo(b, pl.ds(pl.multiple_of(b * rows, 8), rows))
            return carry
        lax.fori_loop(0, 2, body, 0)

    def compact(b, ds):
        mass = state[pl.ds(pl.multiple_of(2 * ROWS * b, 8), ROWS, stride=2), :]
        temper = state[pl.ds(pl.multiple_of(2 * ROWS * b, 8) + 1, ROWS, stride=2), :]
        compact_block(b, ROWS, slot[ds, :], dest[ds, :], cell[ds, :], mass, temper, acc)
    on_blocks(ROWS, compact)
    turned = acc[...].T
    for f in range(4):
        head, tail = turned[32 * f:32 * f + 16, :], turned[32 * f + 16:32 * f + 32, :]
        both = head + tail if f < 2 else head * 256.0 + tail
        if f == 2:
            cell[128:144, :] = both[:, :128].astype(jnp.int32)
            cell[144:160, :] = both[:, 128:].astype(jnp.int32)
        elif f < 2:
            leaver[f, 0:16, :] = both[:, :128]
            leaver[f, 16:32, :] = both[:, 128:]
        else:
            box[0, 3] = both[:8]
            box[1, 3] = both[8:]

    receive_near(0, 0)
    on_rest(lambda i: first(3, i))
    receive_far(0, 3)
    first(3, outer)
    stage(1, 0)
    send_y(1, 0)
    send_near(1, 0)
    send_far(0, 2)
    send_far(1, 3)
    send_far(0, 4)
    receive_near(0, 1)

    def winds(i):
        for f in range(3):
            first(f, i)
    on_rest(winds)
    receive_near(0, 2)
    on_rest(lambda i: first(4, i))

    def second_heat(half):
        def body(n, carry):
            i = n + 2 * half
            t2[i] = plane(g1, hy1, 3, i + 1)
            return carry
        lax.fori_loop(0, 2, body, 0)
        table(t2[pl.ds(2 * half, 2)].reshape(64, 512), tab)

    receive_near(1, 0)
    second_heat(near_half)

    def near_gather(b, ds):
        seen[ds, :] = gather_block(cell[ds, :], near_half, tab)
    on_blocks(80, near_gather)

    receive_far(0, 0, 1, 2)
    winds(outer)
    stage(1, 1)
    send_y(1, 1)
    send_far(1, 0, 1, 2)
    send_near(1, 1)
    receive_far(1, 3)
    second_heat(far_half)

    def far_gather(b, ds):
        seen[ds, :] += gather_block(cell[ds, :], far_half, tab)
    on_blocks(80, far_gather)
    left_over, warm, burned = burn(leaver[0], leaver[1], seen[128:160, :])
    place = lax.broadcasted_iota(jnp.int32, (8, 128), 0) * 256 + lax.broadcasted_iota(jnp.int32, (8, 128), 1)
    for face in range(2):
        for part in range(2):
            lanes = slice(128 * part, 128 * part + 128)
            live = place + 128 * part < counts[0, face]
            at = 16 * part + 8 * face
            for f, v in enumerate((left_over, warm, burned)):
                box[face, f, :, lanes] = jnp.where(live, v[at:at + 8], 0.0)
            box[face, 3, :, lanes] = jnp.where(live, box[face, 3, :, lanes], 0.0)
    down = remote(box.at[0], got.at[1], fs.at[0], fr.at[0], below)
    up = remote(box.at[1], got.at[0], fs.at[1], fr.at[1], above)
    pl.when(has_below)(down.start)
    pl.when(has_above)(up.start)
    receive_far(0, 4)
    first(4, outer)
    stage(1, 2)
    send_y(1, 2)
    send_far(1, 4)
    send_near(1, 2)
    left_over, warm, burned = burn(state[pl.ds(0, 128, stride=2), :], state[pl.ds(1, 128, stride=2), :], seen[0:128, :])
    state_out[pl.ds(0, 128, stride=2), :] = left_over
    state_out[pl.ds(1, 128, stride=2), :] = warm
    stay[...] = jnp.where(slot[...] < 0, burned, 0.0)

    def deposit(b, ds):
        deposit_block(dest[ds, :], stay[ds, :], ROWS, rel)
    on_blocks(ROWS, deposit)

    receive_near(1, 1)

    def later_winds(i):
        for f in range(3):
            second(f, i)
    on_rest(later_winds)
    receive_near(1, 2)
    on_rest(lambda i: second(4, i))
    for f in (0, 1, 2, 4):
        receive_far(1, f)
        second(f, outer)

    pl.when(has_below)(up.wait_recv)
    pl.when(has_above)(down.wait_recv)
    where_to, burned = [], []
    for d in range(2):
        for part in range(2):
            lanes = slice(128 * part, 128 * part + 128)
            where_to.append(got[d, 3, :, lanes].astype(jnp.int32))
            burned.append(got[d, 2, :, lanes])
            for f in range(3):
                arr_out[f, pl.ds(2 * part + d, 8, stride=4), :] = got[d, f, :, lanes]
    deposit_block(jnp.concatenate(where_to, axis=0), jnp.concatenate(burned, axis=0), 32, rel)
    both = rel[:256, :] + rel[256:, :]
    release = jnp.concatenate([both[:128], both[128:]], axis=1).reshape(4, 32, 512)
    gas_out[3] = t2[...] + 1.5 * release
    gas_out[4] = gas_out[4] + release

    @pl.when(has_far)
    def _():
        for r in range(2):
            for f in range(5):
                halo_far(r, f).wait_send()

    for r in range(2):
        for k in range(3):
            halo_near(r, k).wait_send()
    for d, there in ((0, has_left), (1, has_right)):
        @pl.when(there)
        def _():
            for r in range(2):
                for k in range(3):
                    halo_y(r, k, d).wait_send()
    pl.when(has_below)(down.wait_send)
    pl.when(has_above)(up.wait_send)


def write_kernel(gas, state, arr, gas_hbm, state_hbm, arr_hbm, sem):
    copies = [pltpu.make_async_copy(gas.at[f], gas_hbm.at[f], sem.at[f]) for f in range(5)]
    copies += [pltpu.make_async_copy(state, state_hbm, sem.at[5]), pltpu.make_async_copy(arr, arr_hbm, sem.at[6])]
    for copy in copies:
        copy.start()
    for copy in copies:
        copy.wait()


def on_device(gas, parcel_state, parcel_cell, parcel_dest, send_slot, face_counts):
    square = lambda a: a.reshape(128, 128)
    state = parcel_state.reshape(2, 128, 128).transpose(1, 0, 2).reshape(256, 128)
    vm = pl.BlockSpec(memory_space=pltpu.VMEM)
    hbm = pl.BlockSpec(memory_space=pltpu.HBM)
    i32 = lambda *s: pltpu.VMEM(s, jnp.int32)
    f32 = lambda *s: pltpu.VMEM(s, F32)
    dma = pltpu.SemaphoreType.DMA
    inputs = (gas, square(parcel_cell), square(parcel_dest), square(send_slot), state, face_counts.reshape(1, 2))
    gas_out, out, arr = pl.pallas_call(
        step_kernel,
        out_shape=(
            jax.ShapeDtypeStruct(gas.shape, F32),
            jax.ShapeDtypeStruct((256, 128), F32),
            jax.ShapeDtypeStruct((3, 32, 128), F32),
        ),
        in_specs=[hbm] * 6,
        out_specs=(vm, vm, vm),
        scratch_shapes=[
            f32(5, 6, 32, 512), f32(5, 6, 32, 512), f32(4, 32, 512),
            f32(5, 2, 4, 512), f32(5, 2, 4, 512), f32(5, 2, 4, 512), f32(5, 2, 4, 512),
            i32(160, 128), i32(128, 128), i32(128, 128), f32(256, 128), pltpu.SMEM((1, 2), jnp.int32),
            pltpu.VMEM((256, 256), BF), f32(160, 128), f32(2, 32, 128), f32(128, 128), f32(256, 128), f32(512, 256),
            f32(2, 4, 8, 256), f32(2, 4, 8, 256),
            dma((8,)), dma((2, 5)), dma((2, 5)), dma((2, 3)), dma((2, 3)), dma((2, 3, 2)), dma((2, 3, 2)), dma((2,)), dma((2,)),
        ],
        compiler_params=pltpu.CompilerParams(vmem_limit_bytes=44 << 20, collective_id=0, has_side_effects=True),
        name="dust_step",
    )(*[pltpu.with_memory_space_constraint(a, pltpu.HBM) for a in inputs])
    results = (gas_out, out, arr)
    gas_out, out, arr = pl.pallas_call(
        write_kernel,
        out_shape=tuple(jax.ShapeDtypeStruct(a.shape, F32) for a in results),
        in_specs=[vm] * 3,
        out_specs=(hbm, hbm, hbm),
        scratch_shapes=[dma((7,))],
        name="write",
    )(*[pltpu.with_memory_space_constraint(a, pltpu.VMEM) for a in results])
    parcels_out = out.reshape(128, 2, 128).transpose(1, 0, 2).reshape(2, 16384)
    arrivals = arr.reshape(3, 16, 2, 128).transpose(2, 0, 1, 3).reshape(2, 3, 2048)
    return (gas_out, parcels_out, arrivals)


def solution(mesh):
    in_specs = (
        P(None, "prop", "cross", None),
        P(None, ("prop", "cross")),
        P(("prop", "cross")),
        P(("prop", "cross")),
        P(("prop", "cross")),
        P("prop", "cross", None),
    )
    out_specs = (
        P(None, "prop", "cross", None),
        P(None, ("prop", "cross")),
        P(None, None, ("prop", "cross")),
    )
    return jax.shard_map(
        on_device, mesh=mesh, in_specs=in_specs, out_specs=out_specs, check_vma=False
    )
```

```python
import functools
import jax
import jax.numpy as jnp
from jax import lax
from jax.experimental import pallas as pl
from jax.experimental.pallas import tpu as pltpu
from jax.sharding import PartitionSpec as P

F32 = jnp.float32
BF = jnp.bfloat16
ROWS = 64
NT = (((1,), (1,)), ((), ()))
GROUPS = ((3, 4), (0, 3), (4, 5))


def iota_bf(n):
    return lax.broadcasted_iota(jnp.int32, (n, 128), 0).astype(F32).astype(BF)


def wide(row, n):
    t = jnp.broadcast_to(row, (16, 128)).astype(BF)
    return jnp.concatenate([t] * (n // 16), axis=0)


def split(x):
    hi = x.astype(BF).astype(F32)
    return hi, x - hi


def key_of(cell):
    return (((cell >> 8) & 1) * 128 + (cell >> 9)).astype(F32)


def low_of(cell):
    return (cell & 255).astype(F32)


def half_key(cell, half):
    key = ((cell >> 8) & 1) * 64 + ((cell >> 9) & 63)
    return jnp.where((cell >> 15) == half, key, -1).astype(F32)


def table(T, tab_ref):
    hi, lo = split(T)
    m = jnp.concatenate([hi[:, :256], hi[:, 256:], lo[:, :256], lo[:, 256:]], axis=0)
    tab_ref[...] = m.T.astype(BF)


def gather_block(cell, half, tab_ref):
    rows = cell.shape[0]
    key = half_key(cell, half)
    lo = low_of(cell)
    it = iota_bf(128)
    one = jnp.ones((128, 128), BF)
    zero = jnp.zeros((128, 128), BF)
    oh = jnp.concatenate([jnp.where(it == wide(key[i:i + 1], 128), one, zero) for i in range(rows)], axis=1)
    res = jnp.dot(tab_ref[...], jnp.concatenate([oh, oh], axis=0), preferred_element_type=F32)
    itf = lax.broadcasted_iota(jnp.int32, (256, 128), 0).astype(F32)
    out = []
    for i in range(rows):
        r = res[:, i * 128:(i + 1) * 128]
        out.append(jnp.sum(jnp.where(itf == lo[i:i + 1], r, 0.0), axis=0, keepdims=True))
    return jnp.concatenate(out, axis=0)


def burn(mass, temper, seen):
    hot = temper + 0.3 * (seen - temper)
    burned = 0.2 * mass * (1.0 + 0.5 * jnp.tanh(hot))
    return mass - burned, hot + 0.5 * burned, burned


def compact_block(b, rows, slot, dest, cell, mass, temper, acc_ref):
    hi = (slot >> 8).astype(F32)
    lo = (slot & 255).astype(F32)
    vals = [*split(mass), *split(temper)]
    for index in (cell, dest):
        vals += [(index >> 8).astype(F32), (index & 255).astype(F32)]
    it = iota_bf(256)
    it16 = iota_bf(16)
    one = jnp.ones((256, 128), BF)
    zero = jnp.zeros((256, 128), BF)
    z16 = jnp.zeros((16, 128), BF)
    As, Bs = [], []
    for i in range(rows):
        Bs.append(jnp.where(it == wide(lo[i:i + 1], 256), one, zero))
        m = it16 == wide(hi[i:i + 1], 16)
        As.append(jnp.concatenate([jnp.where(m, wide(v[i:i + 1], 16), z16) for v in vals], axis=0))
    A = jnp.concatenate(As, axis=1)
    B = jnp.concatenate(Bs, axis=1)
    acc_ref[...] += lax.dot_general(B, A, NT, preferred_element_type=F32)


def deposit_block(dest, burned, rows):
    hi = key_of(dest)
    lo = low_of(dest)
    bh, bl = split(burned)
    it = iota_bf(256)
    one = jnp.ones((256, 128), BF)
    zero = jnp.zeros((256, 128), BF)
    As, Bs = [], []
    for i in range(rows):
        Bs.append(jnp.where(it == wide(lo[i:i + 1], 256), one, zero))
        m = it == wide(hi[i:i + 1], 256)
        As.append(jnp.concatenate([jnp.where(m, wide(bh[i:i + 1], 256), zero), jnp.where(m, wide(bl[i:i + 1], 256), zero)], axis=0))
    A = jnp.concatenate(As, axis=1)
    B = jnp.concatenate(Bs, axis=1)
    return lax.dot_general(A, B, NT, preferred_element_type=F32)


def plane(g, hy, f, i):
    c = g[f, i]
    rows, depth = c.shape
    row = lax.broadcasted_iota(jnp.int32, (8, depth), 0)
    lane = lax.broadcasted_iota(jnp.int32, (rows, 128), 1)
    xm, xp = g[f, i - 1], g[f, i + 1]
    down, up = pltpu.roll(c, 1, 0), pltpu.roll(c, rows - 1, 0)
    ym = jnp.concatenate([jnp.where(row == 0, hy[f, 0, i - 1], down[:8]), down[8:]], axis=0)
    yp = jnp.concatenate([up[:-8], jnp.where(row == 7, hy[f, 1, i - 1], up[-8:])], axis=0)
    back, on = pltpu.roll(c, 1, 1), pltpu.roll(c, depth - 1, 1)
    zm = jnp.concatenate([jnp.where(lane == 0, 0.0, back[:, :128]), back[:, 128:]], axis=1)
    zp = jnp.concatenate([on[:, :-128], jnp.where(lane == 127, 0.0, on[:, -128:])], axis=1)
    advect = g[0, i] * (xp - xm) + g[1, i] * (yp - ym) + g[2, i] * (zp - zm)
    around = (xp + xm) + (yp + ym) + (zp + zm)
    return (0.28 * c + 0.12 * around) - 0.05 * advect


def step_kernel(gas_hbm, cell_hbm, dest_hbm, slot_hbm, state_hbm, counts_hbm,
                gas_out, state_out, arr_out, come, rel,
                g0, g1, t2, hy0, hy1, sy0, sy1, cell, dest, slot, state, counts,
                tab, seen, leaver, stay, acc, box, got,
                in_sem, fars, farr, xs, xr, ys, yr, hs, hr, fs, fr):
    p, c = lax.axis_index("prop"), lax.axis_index("cross")
    np_, nc = lax.axis_size("prop"), lax.axis_size("cross")
    side = lax.rem(p, 2)
    below = {"prop": lax.rem(p + np_ - 1, np_)}
    above = {"prop": lax.rem(p + 1, np_)}
    near = {"prop": p + 1 - 2 * side}
    far = {"prop": lax.rem(p + np_ - 1 + 2 * side, np_)}
    left = {"cross": lax.rem(c + nc - 1, nc)}
    right = {"cross": lax.rem(c + 1, nc)}
    near_half, far_half = 1 - side, side
    inner, outer, rest = 4 - 3 * side, 1 + 3 * side, 2 - side
    has_below, has_above, has_left, has_right = p > 0, p < np_ - 1, c > 0, c < nc - 1
    edge = jnp.logical_or(p == 0, p == np_ - 1)
    has_far = jnp.logical_not(edge)
    gs, hys, sys_ = (g0, g1), (hy0, hy1), (sy0, sy1)

    def remote(a, b, s, r, to):
        return pltpu.make_async_remote_copy(src_ref=a, dst_ref=b, send_sem=s, recv_sem=r, device_id=to, device_id_type=pl.DeviceIdType.MESH)

    def halo_far(r, f):
        source = gas_hbm.at[f, outer - 1] if r == 0 else g1.at[f, outer]
        return remote(source, gs[r].at[f, 5 * (1 - side)], fars.at[r, f], farr.at[r, f], far)

    def halo_near(r, k):
        lo, hi = GROUPS[k]
        fields = pl.ds(lo, hi - lo)
        source = gas_hbm.at[fields, inner - 1] if r == 0 else g1.at[fields, inner]
        return remote(source, gs[r].at[fields, 5 * side], xs.at[r, k], xr.at[r, k], near)

    def halo_y(r, k, d):
        lo, hi = GROUPS[k]
        fields = pl.ds(lo, hi - lo)
        return remote(sys_[r].at[fields, d], hys[r].at[fields, 1 - d], ys.at[r, k, d], yr.at[r, k, d], right if d else left)

    def heat_y(n, d):
        planes = pl.ds(2 * (far_half if n else near_half), 2)
        return remote(sy1.at[3, d, planes], hy1.at[3, 1 - d, planes], hs.at[n, d], hr.at[n, d], right if d else left)

    def stage_heat(half):
        for n in range(2):
            i = 2 * half + n
            sy1[3, 0, i] = g1[3, 1 + i, 0:1, :]
            sy1[3, 1, i] = g1[3, 1 + i, 31:32, :]

    def send_heat_y(n):
        pl.when(has_left)(lambda: heat_y(n, 0).start())
        pl.when(has_right)(lambda: heat_y(n, 1).start())

    def receive_heat_y(n):
        pl.when(has_left)(lambda: heat_y(n, 1).wait_recv())
        pl.when(has_right)(lambda: heat_y(n, 0).wait_recv())

    def stage(r, k):
        for f in range(*GROUPS[k]):
            for i in range(4):
                sys_[r][f, 0, i] = gs[r][f, 1 + i, 0:1, :]
                sys_[r][f, 1, i] = gs[r][f, 1 + i, 31:32, :]

    def send_far(r, *fields):
        @pl.when(has_far)
        def _():
            for f in fields:
                halo_far(r, f).start()

    def send_near(r, k):
        halo_near(r, k).start()

    def send_y(r, *groups):
        @pl.when(has_left)
        def _():
            for k in groups:
                halo_y(r, k, 0).start()

        @pl.when(has_right)
        def _():
            for k in groups:
                halo_y(r, k, 1).start()

    def receive_near(r, k):
        halo_near(r, k).wait_recv()

        @pl.when(has_left)
        def _():
            halo_y(r, k, 1).wait_recv()

        @pl.when(has_right)
        def _():
            halo_y(r, k, 0).wait_recv()

    def receive_far(r, *fields):
        @pl.when(has_far)
        def _():
            for f in fields:
                halo_far(r, f).wait_recv()

    def first(f, i):
        fresh = plane(g0, hy0, f, i)
        g1[f, i] = fresh + 0.1 * g0[3, i] if f == 2 else fresh

    def second(f, i):
        fresh = plane(g1, hy1, f, i)
        gas_out[f, i - 1] = fresh + 0.1 * g1[3, i] if f == 2 else fresh

    def on_rest(todo):
        for n in range(3):
            todo(rest + n)

    loads = [
        pltpu.make_async_copy(gas_hbm.at[pl.ds(3, 1)], g0.at[pl.ds(3, 1), pl.ds(1, 4)], in_sem.at[0]),
        pltpu.make_async_copy(gas_hbm.at[pl.ds(0, 3)], g0.at[pl.ds(0, 3), pl.ds(1, 4)], in_sem.at[1]),
        pltpu.make_async_copy(gas_hbm.at[pl.ds(4, 1)], g0.at[pl.ds(4, 1), pl.ds(1, 4)], in_sem.at[2]),
        pltpu.make_async_copy(cell_hbm, cell.at[pl.ds(0, 128)], in_sem.at[3]),
        pltpu.make_async_copy(state_hbm, state, in_sem.at[4]),
        pltpu.make_async_copy(slot_hbm, slot, in_sem.at[5]),
        pltpu.make_async_copy(dest_hbm, dest, in_sem.at[6]),
        pltpu.make_async_copy(counts_hbm, counts, in_sem.at[7]),
    ]
    barrier = pltpu.get_barrier_semaphore()
    def greet(to):
        pl.semaphore_signal(barrier, inc=1, device_id=to, device_id_type=pl.DeviceIdType.MESH)

    greet(near)
    pl.when(has_far)(lambda: greet(far))
    pl.when(has_left)(lambda: greet(left))
    pl.when(has_right)(lambda: greet(right))
    for load in loads:
        load.start()

    @pl.when(edge)
    def _():
        for g in gs:
            for f in range(5):
                g[f, 5 * side] = jnp.zeros((32, 512), F32)

    @pl.when(c == 0)
    def _():
        for hy in hys:
            hy[:, 0] = jnp.zeros((5, 4, 1, 512), F32)

    @pl.when(c == nc - 1)
    def _():
        for hy in hys:
            hy[:, 1] = jnp.zeros((5, 4, 1, 512), F32)

    @pl.when(p == 0)
    def _():
        got[0] = jnp.zeros((4, 8, 256), F32)

    @pl.when(p == np_ - 1)
    def _():
        got[1] = jnp.zeros((4, 8, 256), F32)

    loads[0].wait()
    stage(0, 0)
    loads[1].wait()
    stage(0, 1)
    loads[2].wait()
    stage(0, 2)
    pl.semaphore_wait(barrier, 1 + has_far.astype(jnp.int32) + has_left.astype(jnp.int32) + has_right.astype(jnp.int32))
    send_y(0, 0)
    send_far(0, 3)
    send_near(0, 0)
    send_y(0, 1, 2)
    send_far(0, 0, 1)
    send_near(0, 1)
    send_near(0, 2)
    acc[...] = jnp.zeros_like(acc)
    rel[...] = jnp.zeros_like(rel)
    for load in loads[3:]:
        load.wait()

    def on_blocks(rows, todo):
        def body(b, carry):
            todo(b, pl.ds(pl.multiple_of(b * rows, 8), rows))
            return carry
        lax.fori_loop(0, (160 if rows == 160 else 128) // rows, body, 0)

    def compact(b, ds):
        mass = state[pl.ds(pl.multiple_of(2 * ROWS * b, 8), ROWS, stride=2), :]
        temper = state[pl.ds(pl.multiple_of(2 * ROWS * b, 8) + 1, ROWS, stride=2), :]
        compact_block(b, ROWS, slot[ds, :], dest[ds, :], cell[ds, :], mass, temper, acc)
    on_blocks(ROWS, compact)
    turned = acc[...].T
    for f in range(4):
        head, tail = turned[32 * f:32 * f + 16, :], turned[32 * f + 16:32 * f + 32, :]
        both = head + tail if f < 2 else head * 256.0 + tail
        if f == 2:
            cell[128:144, :] = both[:, :128].astype(jnp.int32)
            cell[144:160, :] = both[:, 128:].astype(jnp.int32)
        elif f < 2:
            leaver[f, 0:16, :] = both[:, :128]
            leaver[f, 16:32, :] = both[:, 128:]
        else:
            box[0, 3] = both[:8]
            box[1, 3] = both[8:]

    receive_near(0, 0)
    on_rest(lambda i: first(3, i))
    stage_heat(near_half)
    send_heat_y(0)
    send_near(1, 0)
    send_far(0, 2)
    receive_near(0, 1)

    def winds(i):
        for f in range(3):
            first(f, i)
    on_rest(winds)
    receive_far(0, 3)
    first(3, outer)
    stage_heat(far_half)
    send_heat_y(1)
    send_far(1, 3)
    send_far(0, 4)
    receive_near(0, 2)
    on_rest(lambda i: first(4, i))

    def second_heat(half):
        for n in range(2):
            i = n + 2 * half
            t2[i] = plane(g1, hy1, 3, i + 1)
        table(t2[pl.ds(2 * half, 2)].reshape(64, 512), tab)

    halo_near(1, 0).wait_recv()
    receive_heat_y(0)
    second_heat(near_half)

    def near_gather(b, ds):
        seen[ds, :] = gather_block(cell[ds, :], near_half, tab)
    on_blocks(160, near_gather)

    receive_far(0, 0, 1, 2)
    winds(outer)
    stage(1, 1)
    send_y(1, 1)
    send_far(1, 0, 1, 2)
    send_near(1, 1)
    receive_heat_y(1)
    receive_far(1, 3)
    second_heat(far_half)

    def far_gather(b, ds):
        seen[ds, :] += gather_block(cell[ds, :], far_half, tab)
    on_blocks(160, far_gather)
    left_over, warm, burned = burn(leaver[0], leaver[1], seen[128:160, :])
    place = lax.broadcasted_iota(jnp.int32, (8, 128), 0) * 256 + lax.broadcasted_iota(jnp.int32, (8, 128), 1)
    for face in range(2):
        for part in range(2):
            lanes = slice(128 * part, 128 * part + 128)
            live = place + 128 * part < counts[0, face]
            at = 16 * part + 8 * face
            for f, v in enumerate((left_over, warm, burned)):
                box[face, f, :, lanes] = jnp.where(live, v[at:at + 8], 0.0)
            box[face, 3, :, lanes] = jnp.where(live, box[face, 3, :, lanes], 0.0)
    down = remote(box.at[0], got.at[1], fs.at[0], fr.at[0], below)
    up = remote(box.at[1], got.at[0], fs.at[1], fr.at[1], above)
    pl.when(has_below)(down.start)
    pl.when(has_above)(up.start)
    receive_far(0, 4)
    first(4, outer)
    stage(1, 2)
    send_y(1, 2)
    send_far(1, 4)
    send_near(1, 2)
    left_over, warm, burned = burn(state[pl.ds(0, 128, stride=2), :], state[pl.ds(1, 128, stride=2), :], seen[0:128, :])
    state_out[pl.ds(0, 128, stride=2), :] = left_over
    state_out[pl.ds(1, 128, stride=2), :] = warm
    stay[...] = jnp.where(slot[...] < 0, burned, 0.0)

    def deposit(b, ds):
        rel[...] += deposit_block(dest[ds, :], stay[ds, :], ROWS)
        for n in range(3):
            gas_out[b, rest + n - 1] = plane(g1, hy1, b, rest + n)
    receive_near(1, 1)
    on_blocks(ROWS, deposit)


    on_rest(lambda i: second(2, i))
    receive_near(1, 2)
    on_rest(lambda i: second(4, i))
    for f in (0, 1, 2, 4):
        receive_far(1, f)
        second(f, outer)

    pl.when(has_below)(up.wait_recv)
    pl.when(has_above)(down.wait_recv)
    for d in range(2):
        for part in range(2):
            lanes = slice(128 * part, 128 * part + 128)
            at = 16 * d + 8 * part
            come[0, at:at + 8, :] = got[d, 2, :, lanes]
            come[1, at:at + 8, :] = got[d, 3, :, lanes]
            for f in range(3):
                arr_out[f, pl.ds(2 * part + d, 8, stride=4), :] = got[d, f, :, lanes]
    gas_out[3] = t2[...]

    @pl.when(has_far)
    def _():
        for r in range(2):
            for f in range(5):
                halo_far(r, f).wait_send()

    for r in range(2):
        for k in range(3):
            halo_near(r, k).wait_send()
    for d, there in ((0, has_left), (1, has_right)):
        @pl.when(there)
        def _():
            for r in range(2):
                for k in range(r, 3):
                    halo_y(r, k, d).wait_send()
                heat_y(r, d).wait_send()
    pl.when(has_below)(down.wait_send)
    pl.when(has_above)(up.wait_send)


def write_kernel(gas, state, arr, come, rel, gas_hbm, state_hbm, arr_hbm, last, sem):
    copies = [pltpu.make_async_copy(gas.at[f], gas_hbm.at[f], sem.at[f]) for f in range(3)]
    copies += [pltpu.make_async_copy(state, state_hbm, sem.at[5]), pltpu.make_async_copy(arr, arr_hbm, sem.at[6])]
    for copy in copies:
        copy.start()
    release = rel[...] + deposit_block(come[1].astype(jnp.int32), come[0], 32)
    both = release[:256, :] + release[256:, :]
    release = jnp.concatenate([both[:128], both[128:]], axis=1).reshape(4, 32, 512)
    for n in range(2):
        last[n] = gas[3 + n] + (1.5 * release if n == 0 else release)
        copies.append(pltpu.make_async_copy(last.at[n], gas_hbm.at[3 + n], sem.at[3 + n]))
        copies[-1].start()
    for copy in copies:
        copy.wait()


def on_device(gas, parcel_state, parcel_cell, parcel_dest, send_slot, face_counts):
    square = lambda a: a.reshape(128, 128)
    state = parcel_state.reshape(2, 128, 128).transpose(1, 0, 2).reshape(256, 128)
    vm = pl.BlockSpec(memory_space=pltpu.VMEM)
    hbm = pl.BlockSpec(memory_space=pltpu.HBM)
    i32 = lambda *s: pltpu.VMEM(s, jnp.int32)
    f32 = lambda *s: pltpu.VMEM(s, F32)
    dma = pltpu.SemaphoreType.DMA
    inputs = (gas, square(parcel_cell), square(parcel_dest), square(send_slot), state, face_counts.reshape(1, 2))
    results = pl.pallas_call(
        step_kernel,
        out_shape=(
            jax.ShapeDtypeStruct(gas.shape, F32),
            jax.ShapeDtypeStruct((256, 128), F32),
            jax.ShapeDtypeStruct((3, 32, 128), F32),
            jax.ShapeDtypeStruct((2, 32, 128), F32),
            jax.ShapeDtypeStruct((512, 256), F32),
        ),
        in_specs=[hbm] * 6,
        out_specs=(vm,) * 5,
        scratch_shapes=[
            f32(5, 6, 32, 512), f32(5, 6, 32, 512), f32(4, 32, 512),
            f32(5, 2, 4, 1, 512), f32(5, 2, 4, 1, 512), f32(5, 2, 4, 1, 512), f32(5, 2, 4, 1, 512),
            i32(160, 128), i32(128, 128), i32(128, 128), f32(256, 128), pltpu.SMEM((1, 2), jnp.int32),
            pltpu.VMEM((256, 256), BF), f32(160, 128), f32(2, 32, 128), f32(128, 128), f32(256, 128),
            f32(2, 4, 8, 256), f32(2, 4, 8, 256),
            dma((8,)), dma((2, 5)), dma((2, 5)), dma((2, 3)), dma((2, 3)), dma((2, 3, 2)), dma((2, 3, 2)), dma((2, 2)), dma((2, 2)), dma((2,)), dma((2,)),
        ],
        compiler_params=pltpu.CompilerParams(vmem_limit_bytes=44 << 20, collective_id=0, has_side_effects=True),
        name="dust_step",
    )(*[pltpu.with_memory_space_constraint(a, pltpu.HBM) for a in inputs])
    gas_out, out, arr = pl.pallas_call(
        write_kernel,
        out_shape=tuple(jax.ShapeDtypeStruct(a.shape, F32) for a in results[:3]),
        in_specs=[vm] * 5,
        out_specs=(hbm, hbm, hbm),
        scratch_shapes=[f32(2, 4, 32, 512), dma((7,))],
        compiler_params=pltpu.CompilerParams(vmem_limit_bytes=16 << 20),
        name="write",
    )(*[pltpu.with_memory_space_constraint(a, pltpu.VMEM) for a in results])
    parcels_out = out.reshape(128, 2, 128).transpose(1, 0, 2).reshape(2, 16384)
    arrivals = arr.reshape(3, 16, 2, 128).transpose(2, 0, 1, 3).reshape(2, 3, 2048)
    return (gas_out, parcels_out, arrivals)


def solution(mesh):
    in_specs = (
        P(None, "prop", "cross", None),
        P(None, ("prop", "cross")),
        P(("prop", "cross")),
        P(("prop", "cross")),
        P(("prop", "cross")),
        P("prop", "cross", None),
    )
    out_specs = (
        P(None, "prop", "cross", None),
        P(None, ("prop", "cross")),
        P(None, None, ("prop", "cross")),
    )
    return jax.shard_map(
        on_device, mesh=mesh, in_specs=in_specs, out_specs=out_specs, check_vma=False
    )
```

```python
import functools
import jax
import jax.numpy as jnp
from jax import lax
from jax.experimental import pallas as pl
from jax.experimental.pallas import tpu as pltpu
from jax.sharding import PartitionSpec as P

F32 = jnp.float32
BF = jnp.bfloat16
ROWS = 64
NT = (((1,), (1,)), ((), ()))
GROUPS = ((3, 4), (0, 3), (4, 5))


def iota_bf(n):
    return lax.broadcasted_iota(jnp.int32, (n, 128), 0).astype(F32).astype(BF)


def wide(row, n):
    t = jnp.broadcast_to(row, (16, 128)).astype(BF)
    return jnp.concatenate([t] * (n // 16), axis=0)


def split(x):
    hi = x.astype(BF).astype(F32)
    return hi, x - hi


def key_of(cell):
    return (((cell >> 8) & 1) * 128 + (cell >> 9)).astype(F32)


def low_of(cell):
    return (cell & 255).astype(F32)


def half_key(cell, half):
    key = ((cell >> 8) & 1) * 64 + ((cell >> 9) & 63)
    return jnp.where((cell >> 15) == half, key, -1).astype(F32)


def table(T, tab_ref):
    hi, lo = split(T)
    m = jnp.concatenate([hi[:, :256], hi[:, 256:], lo[:, :256], lo[:, 256:]], axis=0)
    tab_ref[...] = m.T.astype(BF)


def gather_block(cell, half, tab_ref):
    rows = cell.shape[0]
    key = half_key(cell, half)
    lo = low_of(cell)
    it = iota_bf(128)
    one = jnp.ones((128, 128), BF)
    zero = jnp.zeros((128, 128), BF)
    oh = jnp.concatenate([jnp.where(it == wide(key[i:i + 1], 128), one, zero) for i in range(rows)], axis=1)
    res = jnp.dot(tab_ref[...], jnp.concatenate([oh, oh], axis=0), preferred_element_type=F32)
    itf = lax.broadcasted_iota(jnp.int32, (256, 128), 0).astype(F32)
    out = []
    for i in range(rows):
        r = res[:, i * 128:(i + 1) * 128]
        out.append(jnp.sum(jnp.where(itf == lo[i:i + 1], r, 0.0), axis=0, keepdims=True))
    return jnp.concatenate(out, axis=0)


def burn(mass, temper, seen):
    hot = temper + 0.3 * (seen - temper)
    burned = 0.2 * mass * (1.0 + 0.5 * jnp.tanh(hot))
    return mass - burned, hot + 0.5 * burned, burned


def compact_block(b, rows, slot, dest, cell, mass, temper, acc_ref):
    hi = (slot >> 8).astype(F32)
    lo = (slot & 255).astype(F32)
    vals = [*split(mass), *split(temper)]
    for index in (cell, dest):
        vals += [(index >> 8).astype(F32), (index & 255).astype(F32)]
    it = iota_bf(256)
    it16 = iota_bf(16)
    one = jnp.ones((256, 128), BF)
    zero = jnp.zeros((256, 128), BF)
    z16 = jnp.zeros((16, 128), BF)
    As, Bs = [], []
    for i in range(rows):
        Bs.append(jnp.where(it == wide(lo[i:i + 1], 256), one, zero))
        m = it16 == wide(hi[i:i + 1], 16)
        As.append(jnp.concatenate([jnp.where(m, wide(v[i:i + 1], 16), z16) for v in vals], axis=0))
    A = jnp.concatenate(As, axis=1)
    B = jnp.concatenate(Bs, axis=1)
    acc_ref[...] += lax.dot_general(B, A, NT, preferred_element_type=F32)


def deposit_block(dest, burned, rows):
    hi = key_of(dest)
    lo = low_of(dest)
    bh, bl = split(burned)
    it = iota_bf(256)
    one = jnp.ones((256, 128), BF)
    zero = jnp.zeros((256, 128), BF)
    As, Bs = [], []
    for i in range(rows):
        Bs.append(jnp.where(it == wide(lo[i:i + 1], 256), one, zero))
        m = it == wide(hi[i:i + 1], 256)
        As.append(jnp.concatenate([jnp.where(m, wide(bh[i:i + 1], 256), zero), jnp.where(m, wide(bl[i:i + 1], 256), zero)], axis=0))
    A = jnp.concatenate(As, axis=1)
    B = jnp.concatenate(Bs, axis=1)
    return lax.dot_general(A, B, NT, preferred_element_type=F32)


def plane(g, hy, f, i):
    c = g[f, i]
    rows, depth = c.shape
    row = lax.broadcasted_iota(jnp.int32, (8, depth), 0)
    lane = lax.broadcasted_iota(jnp.int32, (rows, 128), 1)
    xm, xp = g[f, i - 1], g[f, i + 1]
    down, up = pltpu.roll(c, 1, 0), pltpu.roll(c, rows - 1, 0)
    ym = jnp.concatenate([jnp.where(row == 0, hy[f, 0, i - 1], down[:8]), down[8:]], axis=0)
    yp = jnp.concatenate([up[:-8], jnp.where(row == 7, hy[f, 1, i - 1], up[-8:])], axis=0)
    back, on = pltpu.roll(c, 1, 1), pltpu.roll(c, depth - 1, 1)
    zm = jnp.concatenate([jnp.where(lane == 0, 0.0, back[:, :128]), back[:, 128:]], axis=1)
    zp = jnp.concatenate([on[:, :-128], jnp.where(lane == 127, 0.0, on[:, -128:])], axis=1)
    advect = g[0, i] * (xp - xm) + g[1, i] * (yp - ym) + g[2, i] * (zp - zm)
    around = (xp + xm) + (yp + ym) + (zp + zm)
    return (0.28 * c + 0.12 * around) - 0.05 * advect


def step_kernel(gas_hbm, cell_hbm, dest_hbm, slot_hbm, state_hbm, counts_hbm,
                gas_out, state_out, arr_out, come, rel,
                g0, g1, t2, hy0, hy1, sy0, sy1, cell, dest, slot, state, counts,
                tab, seen, leaver, stay, acc, box, got,
                in_sem, fars, farr, xs, xr, ys, yr, hs, hr, fs, fr):
    p, c = lax.axis_index("prop"), lax.axis_index("cross")
    np_, nc = lax.axis_size("prop"), lax.axis_size("cross")
    side = lax.rem(p, 2)
    below = {"prop": lax.rem(p + np_ - 1, np_)}
    above = {"prop": lax.rem(p + 1, np_)}
    near = {"prop": p + 1 - 2 * side}
    far = {"prop": lax.rem(p + np_ - 1 + 2 * side, np_)}
    left = {"cross": lax.rem(c + nc - 1, nc)}
    right = {"cross": lax.rem(c + 1, nc)}
    near_half, far_half = 1 - side, side
    inner, outer, rest = 4 - 3 * side, 1 + 3 * side, 2 - side
    has_below, has_above, has_left, has_right = p > 0, p < np_ - 1, c > 0, c < nc - 1
    edge = jnp.logical_or(p == 0, p == np_ - 1)
    has_far = jnp.logical_not(edge)
    gs, hys, sys_ = (g0, g1), (hy0, hy1), (sy0, sy1)

    def remote(a, b, s, r, to):
        return pltpu.make_async_remote_copy(src_ref=a, dst_ref=b, send_sem=s, recv_sem=r, device_id=to, device_id_type=pl.DeviceIdType.MESH)

    def halo_far(r, f):
        source = gas_hbm.at[f, outer - 1] if r == 0 else g1.at[f, outer]
        return remote(source, gs[r].at[f, 5 * (1 - side)], fars.at[r, f], farr.at[r, f], far)

    def halo_near(r, k):
        lo, hi = GROUPS[k]
        fields = pl.ds(lo, hi - lo)
        source = gas_hbm.at[fields, inner - 1] if r == 0 else g1.at[fields, inner]
        return remote(source, gs[r].at[fields, 5 * side], xs.at[r, k], xr.at[r, k], near)

    def halo_y(r, k, d):
        lo, hi = GROUPS[k]
        fields = pl.ds(lo, hi - lo)
        return remote(sys_[r].at[fields, d], hys[r].at[fields, 1 - d], ys.at[r, k, d], yr.at[r, k, d], right if d else left)

    def heat_y(n, d):
        planes = pl.ds(2 * (far_half if n else near_half), 2)
        return remote(sy1.at[3, d, planes], hy1.at[3, 1 - d, planes], hs.at[n, d], hr.at[n, d], right if d else left)

    def stage_heat(half):
        for n in range(2):
            i = 2 * half + n
            sy1[3, 0, i] = g1[3, 1 + i, 0:1, :]
            sy1[3, 1, i] = g1[3, 1 + i, 31:32, :]

    def send_heat_y(n):
        pl.when(has_left)(lambda: heat_y(n, 0).start())
        pl.when(has_right)(lambda: heat_y(n, 1).start())

    def receive_heat_y(n):
        pl.when(has_left)(lambda: heat_y(n, 1).wait_recv())
        pl.when(has_right)(lambda: heat_y(n, 0).wait_recv())

    def stage(r, k):
        for f in range(*GROUPS[k]):
            for i in range(4):
                sys_[r][f, 0, i] = gs[r][f, 1 + i, 0:1, :]
                sys_[r][f, 1, i] = gs[r][f, 1 + i, 31:32, :]

    def send_far(r, *fields):
        @pl.when(has_far)
        def _():
            for f in fields:
                halo_far(r, f).start()

    def send_near(r, k):
        halo_near(r, k).start()

    def send_y(r, *groups):
        @pl.when(has_left)
        def _():
            for k in groups:
                halo_y(r, k, 0).start()

        @pl.when(has_right)
        def _():
            for k in groups:
                halo_y(r, k, 1).start()

    def receive_near(r, k):
        halo_near(r, k).wait_recv()

        @pl.when(has_left)
        def _():
            halo_y(r, k, 1).wait_recv()

        @pl.when(has_right)
        def _():
            halo_y(r, k, 0).wait_recv()

    def receive_far(r, *fields):
        @pl.when(has_far)
        def _():
            for f in fields:
                halo_far(r, f).wait_recv()

    def first(f, i):
        fresh = plane(g0, hy0, f, i)
        g1[f, i] = fresh + 0.1 * g0[3, i] if f == 2 else fresh

    def second(f, i):
        fresh = plane(g1, hy1, f, i)
        gas_out[f, i - 1] = fresh + 0.1 * g1[3, i] if f == 2 else fresh

    def on_rest(todo):
        for n in range(3):
            todo(rest + n)

    loads = [
        pltpu.make_async_copy(gas_hbm.at[pl.ds(3, 1)], g0.at[pl.ds(3, 1), pl.ds(1, 4)], in_sem.at[0]),
        pltpu.make_async_copy(gas_hbm.at[pl.ds(0, 3)], g0.at[pl.ds(0, 3), pl.ds(1, 4)], in_sem.at[1]),
        pltpu.make_async_copy(gas_hbm.at[pl.ds(4, 1)], g0.at[pl.ds(4, 1), pl.ds(1, 4)], in_sem.at[2]),
        pltpu.make_async_copy(cell_hbm, cell.at[pl.ds(0, 128)], in_sem.at[3]),
        pltpu.make_async_copy(state_hbm, state, in_sem.at[4]),
        pltpu.make_async_copy(slot_hbm, slot, in_sem.at[5]),
        pltpu.make_async_copy(dest_hbm, dest, in_sem.at[6]),
        pltpu.make_async_copy(counts_hbm, counts, in_sem.at[7]),
    ]
    barrier = pltpu.get_barrier_semaphore()
    def greet(to):
        pl.semaphore_signal(barrier, inc=1, device_id=to, device_id_type=pl.DeviceIdType.MESH)

    greet(near)
    pl.when(has_far)(lambda: greet(far))
    pl.when(has_left)(lambda: greet(left))
    pl.when(has_right)(lambda: greet(right))
    for load in loads:
        load.start()

    @pl.when(edge)
    def _():
        for g in gs:
            for f in range(5):
                g[f, 5 * side] = jnp.zeros((32, 512), F32)

    @pl.when(c == 0)
    def _():
        for hy in hys:
            hy[:, 0] = jnp.zeros((5, 4, 1, 512), F32)

    @pl.when(c == nc - 1)
    def _():
        for hy in hys:
            hy[:, 1] = jnp.zeros((5, 4, 1, 512), F32)

    @pl.when(p == 0)
    def _():
        got[0] = jnp.zeros((4, 8, 256), F32)

    @pl.when(p == np_ - 1)
    def _():
        got[1] = jnp.zeros((4, 8, 256), F32)

    loads[0].wait()
    stage(0, 0)
    loads[1].wait()
    stage(0, 1)
    loads[2].wait()
    stage(0, 2)
    pl.semaphore_wait(barrier, 1 + has_far.astype(jnp.int32) + has_left.astype(jnp.int32) + has_right.astype(jnp.int32))
    send_y(0, 0)
    send_far(0, 3)
    send_near(0, 0)
    send_y(0, 1, 2)
    send_far(0, 0)
    send_near(0, 1)
    send_near(0, 2)
    acc[...] = jnp.zeros_like(acc)
    rel[...] = jnp.zeros_like(rel)
    for load in loads[3:]:
        load.wait()

    def on_blocks(rows, todo):
        def body(b, carry):
            todo(b, pl.ds(pl.multiple_of(b * rows, 8), rows))
            return carry
        lax.fori_loop(0, (160 if rows == 160 else 128) // rows, body, 0)

    def compact(b, ds):
        mass = state[pl.ds(pl.multiple_of(2 * ROWS * b, 8), ROWS, stride=2), :]
        temper = state[pl.ds(pl.multiple_of(2 * ROWS * b, 8) + 1, ROWS, stride=2), :]
        compact_block(b, ROWS, slot[ds, :], dest[ds, :], cell[ds, :], mass, temper, acc)
    on_blocks(ROWS, compact)
    turned = acc[...].T
    for f in range(4):
        head, tail = turned[32 * f:32 * f + 16, :], turned[32 * f + 16:32 * f + 32, :]
        both = head + tail if f < 2 else head * 256.0 + tail
        if f == 2:
            cell[128:144, :] = both[:, :128].astype(jnp.int32)
            cell[144:160, :] = both[:, 128:].astype(jnp.int32)
        elif f < 2:
            leaver[f, 0:16, :] = both[:, :128]
            leaver[f, 16:32, :] = both[:, 128:]
        else:
            box[0, 3] = both[:8]
            box[1, 3] = both[8:]

    receive_near(0, 0)
    on_rest(lambda i: first(3, i))
    stage_heat(near_half)
    send_heat_y(0)
    send_near(1, 0)
    send_far(0, 1, 2)
    receive_near(0, 1)

    def winds(i):
        for f in range(3):
            first(f, i)
    on_rest(winds)
    receive_far(0, 3)
    first(3, outer)
    stage_heat(far_half)
    send_heat_y(1)
    send_far(1, 3)
    send_far(0, 4)
    receive_near(0, 2)
    on_rest(lambda i: first(4, i))

    def second_heat(half):
        for n in range(2):
            i = n + 2 * half
            t2[i] = plane(g1, hy1, 3, i + 1)
        table(t2[pl.ds(2 * half, 2)].reshape(64, 512), tab)

    halo_near(1, 0).wait_recv()
    receive_heat_y(0)
    second_heat(near_half)

    def near_gather(b, ds):
        seen[ds, :] = gather_block(cell[ds, :], near_half, tab)
    on_blocks(160, near_gather)

    receive_far(0, 0, 1, 2)
    winds(outer)
    stage(1, 1)
    send_y(1, 1)
    send_far(1, 0, 1, 2)
    send_near(1, 1)
    receive_heat_y(1)
    receive_far(1, 3)
    second_heat(far_half)

    def far_gather(b, ds):
        seen[ds, :] += gather_block(cell[ds, :], far_half, tab)
    on_blocks(160, far_gather)
    left_over, warm, burned = burn(leaver[0], leaver[1], seen[128:160, :])
    place = lax.broadcasted_iota(jnp.int32, (8, 128), 0) * 256 + lax.broadcasted_iota(jnp.int32, (8, 128), 1)
    for face in range(2):
        for part in range(2):
            lanes = slice(128 * part, 128 * part + 128)
            live = place + 128 * part < counts[0, face]
            at = 16 * part + 8 * face
            for f, v in enumerate((left_over, warm, burned)):
                box[face, f, :, lanes] = jnp.where(live, v[at:at + 8], 0.0)
            box[face, 3, :, lanes] = jnp.where(live, box[face, 3, :, lanes], 0.0)
    down = remote(box.at[0], got.at[1], fs.at[0], fr.at[0], below)
    up = remote(box.at[1], got.at[0], fs.at[1], fr.at[1], above)
    pl.when(has_below)(down.start)
    pl.when(has_above)(up.start)
    receive_far(0, 4)
    first(4, outer)
    stage(1, 2)
    send_y(1, 2)
    send_far(1, 4)
    send_near(1, 2)
    left_over, warm, burned = burn(state[pl.ds(0, 128, stride=2), :], state[pl.ds(1, 128, stride=2), :], seen[0:128, :])
    state_out[pl.ds(0, 128, stride=2), :] = left_over
    state_out[pl.ds(1, 128, stride=2), :] = warm
    stay[...] = jnp.where(slot[...] < 0, burned, 0.0)

    def deposit(b, ds):
        rel[...] += deposit_block(dest[ds, :], stay[ds, :], ROWS)
        for n in range(3):
            gas_out[b, rest + n - 1] = plane(g1, hy1, b, rest + n)
    receive_near(1, 1)
    on_blocks(ROWS, deposit)


    on_rest(lambda i: second(2, i))
    receive_near(1, 2)
    on_rest(lambda i: second(4, i))
    for f in (0, 1, 2, 4):
        receive_far(1, f)
        second(f, outer)

    pl.when(has_below)(up.wait_recv)
    pl.when(has_above)(down.wait_recv)
    for d in range(2):
        for part in range(2):
            lanes = slice(128 * part, 128 * part + 128)
            at = 16 * d + 8 * part
            come[0, at:at + 8, :] = got[d, 2, :, lanes]
            come[1, at:at + 8, :] = got[d, 3, :, lanes]
            for f in range(3):
                arr_out[f, pl.ds(2 * part + d, 8, stride=4), :] = got[d, f, :, lanes]
    gas_out[3] = t2[...]

    @pl.when(has_far)
    def _():
        for r in range(2):
            for f in range(5):
                halo_far(r, f).wait_send()

    for r in range(2):
        for k in range(3):
            halo_near(r, k).wait_send()
    for d, there in ((0, has_left), (1, has_right)):
        @pl.when(there)
        def _():
            for r in range(2):
                for k in range(r, 3):
                    halo_y(r, k, d).wait_send()
                heat_y(r, d).wait_send()
    pl.when(has_below)(down.wait_send)
    pl.when(has_above)(up.wait_send)


def write_kernel(gas, state, arr, come, rel, gas_hbm, state_hbm, arr_hbm, last, sem):
    copies = [pltpu.make_async_copy(gas.at[f], gas_hbm.at[f], sem.at[f]) for f in range(3)]
    copies += [pltpu.make_async_copy(state, state_hbm, sem.at[5]), pltpu.make_async_copy(arr, arr_hbm, sem.at[6])]
    for copy in copies:
        copy.start()
    release = rel[...] + deposit_block(come[1].astype(jnp.int32), come[0], 32)
    both = release[:256, :] + release[256:, :]
    release = jnp.concatenate([both[:128], both[128:]], axis=1).reshape(4, 32, 512)
    for n in range(2):
        last[n] = gas[3 + n] + (1.5 * release if n == 0 else release)
        copies.append(pltpu.make_async_copy(last.at[n], gas_hbm.at[3 + n], sem.at[3 + n]))
        copies[-1].start()
    for copy in copies:
        copy.wait()


def on_device(gas, parcel_state, parcel_cell, parcel_dest, send_slot, face_counts):
    square = lambda a: a.reshape(128, 128)
    state = parcel_state.reshape(2, 128, 128).transpose(1, 0, 2).reshape(256, 128)
    vm = pl.BlockSpec(memory_space=pltpu.VMEM)
    hbm = pl.BlockSpec(memory_space=pltpu.HBM)
    i32 = lambda *s: pltpu.VMEM(s, jnp.int32)
    f32 = lambda *s: pltpu.VMEM(s, F32)
    dma = pltpu.SemaphoreType.DMA
    inputs = (gas, square(parcel_cell), square(parcel_dest), square(send_slot), state, face_counts.reshape(1, 2))
    results = pl.pallas_call(
        step_kernel,
        out_shape=(
            jax.ShapeDtypeStruct(gas.shape, F32),
            jax.ShapeDtypeStruct((256, 128), F32),
            jax.ShapeDtypeStruct((3, 32, 128), F32),
            jax.ShapeDtypeStruct((2, 32, 128), F32),
            jax.ShapeDtypeStruct((512, 256), F32),
        ),
        in_specs=[hbm] * 6,
        out_specs=(vm,) * 5,
        scratch_shapes=[
            f32(5, 6, 32, 512), f32(5, 6, 32, 512), f32(4, 32, 512),
            f32(5, 2, 4, 1, 512), f32(5, 2, 4, 1, 512), f32(5, 2, 4, 1, 512), f32(5, 2, 4, 1, 512),
            i32(160, 128), i32(128, 128), i32(128, 128), f32(256, 128), pltpu.SMEM((1, 2), jnp.int32),
            pltpu.VMEM((256, 256), BF), f32(160, 128), f32(2, 32, 128), f32(128, 128), f32(256, 128),
            f32(2, 4, 8, 256), f32(2, 4, 8, 256),
            dma((8,)), dma((2, 5)), dma((2, 5)), dma((2, 3)), dma((2, 3)), dma((2, 3, 2)), dma((2, 3, 2)), dma((2, 2)), dma((2, 2)), dma((2,)), dma((2,)),
        ],
        compiler_params=pltpu.CompilerParams(vmem_limit_bytes=44 << 20, collective_id=0, has_side_effects=True),
        name="dust_step",
    )(*[pltpu.with_memory_space_constraint(a, pltpu.HBM) for a in inputs])
    gas_out, out, arr = pl.pallas_call(
        write_kernel,
        out_shape=tuple(jax.ShapeDtypeStruct(a.shape, F32) for a in results[:3]),
        in_specs=[vm] * 5,
        out_specs=(hbm, hbm, hbm),
        scratch_shapes=[f32(2, 4, 32, 512), dma((7,))],
        compiler_params=pltpu.CompilerParams(vmem_limit_bytes=16 << 20),
        name="write",
    )(*[pltpu.with_memory_space_constraint(a, pltpu.VMEM) for a in results])
    parcels_out = out.reshape(128, 2, 128).transpose(1, 0, 2).reshape(2, 16384)
    arrivals = arr.reshape(3, 16, 2, 128).transpose(2, 0, 1, 3).reshape(2, 3, 2048)
    return (gas_out, parcels_out, arrivals)


def solution(mesh):
    in_specs = (
        P(None, "prop", "cross", None),
        P(None, ("prop", "cross")),
        P(("prop", "cross")),
        P(("prop", "cross")),
        P(("prop", "cross")),
        P("prop", "cross", None),
    )
    out_specs = (
        P(None, "prop", "cross", None),
        P(None, ("prop", "cross")),
        P(None, None, ("prop", "cross")),
    )
    return jax.shard_map(
        on_device, mesh=mesh, in_specs=in_specs, out_specs=out_specs, check_vma=False
    )
```

```python
import functools
import jax
import jax.numpy as jnp
from jax import lax
from jax.experimental import pallas as pl
from jax.experimental.pallas import tpu as pltpu
from jax.sharding import PartitionSpec as P

F32 = jnp.float32
BF = jnp.bfloat16
ROWS = 64
NT = (((1,), (1,)), ((), ()))
GROUPS = ((3, 4), (0, 3), (4, 5))


def iota_bf(n):
    return lax.broadcasted_iota(jnp.int32, (n, 128), 0).astype(F32).astype(BF)


def wide(row, n):
    t = jnp.broadcast_to(row, (16, 128)).astype(BF)
    return jnp.concatenate([t] * (n // 16), axis=0)


def split(x):
    hi = x.astype(BF).astype(F32)
    return hi, x - hi


def key_of(cell):
    return (((cell >> 8) & 1) * 128 + (cell >> 9)).astype(F32)


def low_of(cell):
    return (cell & 255).astype(F32)


def half_key(cell, half):
    key = ((cell >> 8) & 1) * 64 + ((cell >> 9) & 63)
    return jnp.where((cell >> 15) == half, key, -1).astype(F32)


def table(T, tab_ref):
    hi, lo = split(T)
    m = jnp.concatenate([hi[:, :256], hi[:, 256:], lo[:, :256], lo[:, 256:]], axis=0)
    tab_ref[...] = m.T.astype(BF)


def gather_block(cell, half, tab_ref):
    rows = cell.shape[0]
    key = half_key(cell, half)
    lo = low_of(cell)
    it = iota_bf(128)
    one = jnp.ones((128, 128), BF)
    zero = jnp.zeros((128, 128), BF)
    oh = jnp.concatenate([jnp.where(it == wide(key[i:i + 1], 128), one, zero) for i in range(rows)], axis=1)
    res = jnp.dot(tab_ref[...], jnp.concatenate([oh, oh], axis=0), preferred_element_type=F32)
    itf = lax.broadcasted_iota(jnp.int32, (256, 128), 0).astype(F32)
    out = []
    for i in range(rows):
        r = res[:, i * 128:(i + 1) * 128]
        out.append(jnp.sum(jnp.where(itf == lo[i:i + 1], r, 0.0), axis=0, keepdims=True))
    return jnp.concatenate(out, axis=0)


def burn(mass, temper, seen):
    hot = temper + 0.3 * (seen - temper)
    burned = 0.2 * mass * (1.0 + 0.5 * jnp.tanh(hot))
    return mass - burned, hot + 0.5 * burned, burned


def compact_block(b, rows, slot, dest, cell, mass, temper, acc_ref):
    hi = (slot >> 8).astype(F32)
    lo = (slot & 255).astype(F32)
    vals = [*split(mass), *split(temper)]
    for index in (cell, dest):
        vals += [(index >> 8).astype(F32), (index & 255).astype(F32)]
    it = iota_bf(256)
    it16 = iota_bf(16)
    one = jnp.ones((256, 128), BF)
    zero = jnp.zeros((256, 128), BF)
    z16 = jnp.zeros((16, 128), BF)
    As, Bs = [], []
    for i in range(rows):
        Bs.append(jnp.where(it == wide(lo[i:i + 1], 256), one, zero))
        m = it16 == wide(hi[i:i + 1], 16)
        As.append(jnp.concatenate([jnp.where(m, wide(v[i:i + 1], 16), z16) for v in vals], axis=0))
    A = jnp.concatenate(As, axis=1)
    B = jnp.concatenate(Bs, axis=1)
    acc_ref[...] += lax.dot_general(B, A, NT, preferred_element_type=F32)


def deposit_block(dest, burned, rows):
    hi = key_of(dest)
    lo = low_of(dest)
    bh, bl = split(burned)
    it = iota_bf(256)
    one = jnp.ones((256, 128), BF)
    zero = jnp.zeros((256, 128), BF)
    As, Bs = [], []
    for i in range(rows):
        Bs.append(jnp.where(it == wide(lo[i:i + 1], 256), one, zero))
        m = it == wide(hi[i:i + 1], 256)
        As.append(jnp.concatenate([jnp.where(m, wide(bh[i:i + 1], 256), zero), jnp.where(m, wide(bl[i:i + 1], 256), zero)], axis=0))
    A = jnp.concatenate(As, axis=1)
    B = jnp.concatenate(Bs, axis=1)
    return lax.dot_general(A, B, NT, preferred_element_type=F32)


def plane(g, hy, f, i):
    c = g[f, i]
    rows, depth = c.shape
    row = lax.broadcasted_iota(jnp.int32, (8, depth), 0)
    lane = lax.broadcasted_iota(jnp.int32, (rows, 128), 1)
    xm, xp = g[f, i - 1], g[f, i + 1]
    down, up = pltpu.roll(c, 1, 0), pltpu.roll(c, rows - 1, 0)
    ym = jnp.concatenate([jnp.where(row == 0, hy[f, 0, i - 1], down[:8]), down[8:]], axis=0)
    yp = jnp.concatenate([up[:-8], jnp.where(row == 7, hy[f, 1, i - 1], up[-8:])], axis=0)
    back, on = pltpu.roll(c, 1, 1), pltpu.roll(c, depth - 1, 1)
    zm = jnp.concatenate([jnp.where(lane == 0, 0.0, back[:, :128]), back[:, 128:]], axis=1)
    zp = jnp.concatenate([on[:, :-128], jnp.where(lane == 127, 0.0, on[:, -128:])], axis=1)
    advect = g[0, i] * (xp - xm) + g[1, i] * (yp - ym) + g[2, i] * (zp - zm)
    around = (xp + xm) + (yp + ym) + (zp + zm)
    return (0.28 * c + 0.12 * around) - 0.05 * advect


def step_kernel(gas_hbm, cell_hbm, dest_hbm, slot_hbm, state_hbm, counts_hbm,
                gas_out, state_out, arr_out, come, rel,
                g0, g1, t2, hy0, hy1, sy0, sy1, cell, dest, slot, state, counts,
                tab, seen, leaver, stay, acc, box, got,
                in_sem, fars, farr, xs, xr, ys, yr, hs, hr, fs, fr):
    p, c = lax.axis_index("prop"), lax.axis_index("cross")
    np_, nc = lax.axis_size("prop"), lax.axis_size("cross")
    side = lax.rem(p, 2)
    below = {"prop": lax.rem(p + np_ - 1, np_)}
    above = {"prop": lax.rem(p + 1, np_)}
    near = {"prop": p + 1 - 2 * side}
    far = {"prop": lax.rem(p + np_ - 1 + 2 * side, np_)}
    left = {"cross": lax.rem(c + nc - 1, nc)}
    right = {"cross": lax.rem(c + 1, nc)}
    near_half, far_half = 1 - side, side
    inner, outer, rest = 4 - 3 * side, 1 + 3 * side, 2 - side
    has_below, has_above, has_left, has_right = p > 0, p < np_ - 1, c > 0, c < nc - 1
    edge = jnp.logical_or(p == 0, p == np_ - 1)
    has_far = jnp.logical_not(edge)
    gs, hys, sys_ = (g0, g1), (hy0, hy1), (sy0, sy1)

    def remote(a, b, s, r, to):
        return pltpu.make_async_remote_copy(src_ref=a, dst_ref=b, send_sem=s, recv_sem=r, device_id=to, device_id_type=pl.DeviceIdType.MESH)

    def halo_far(r, f):
        source = gas_hbm.at[f, outer - 1] if r == 0 else g1.at[f, outer]
        return remote(source, gs[r].at[f, 5 * (1 - side)], fars.at[r, f], farr.at[r, f], far)

    def halo_near(r, k):
        lo, hi = GROUPS[k]
        fields = pl.ds(lo, hi - lo)
        source = gas_hbm.at[fields, inner - 1] if r == 0 else g1.at[fields, inner]
        return remote(source, gs[r].at[fields, 5 * side], xs.at[r, k], xr.at[r, k], near)

    def halo_y(r, k, d):
        lo, hi = GROUPS[k]
        fields = pl.ds(lo, hi - lo)
        return remote(sys_[r].at[fields, d], hys[r].at[fields, 1 - d], ys.at[r, k, d], yr.at[r, k, d], right if d else left)

    def heat_y(n, d):
        planes = pl.ds(2 * (far_half if n else near_half), 2)
        return remote(sy1.at[3, d, planes], hy1.at[3, 1 - d, planes], hs.at[n, d], hr.at[n, d], right if d else left)

    def stage_heat(half):
        for n in range(2):
            i = 2 * half + n
            sy1[3, 0, i] = g1[3, 1 + i, 0:1, :]
            sy1[3, 1, i] = g1[3, 1 + i, 31:32, :]

    def send_heat_y(n):
        pl.when(has_left)(lambda: heat_y(n, 0).start())
        pl.when(has_right)(lambda: heat_y(n, 1).start())

    def receive_heat_y(n):
        pl.when(has_left)(lambda: heat_y(n, 1).wait_recv())
        pl.when(has_right)(lambda: heat_y(n, 0).wait_recv())

    def stage(r, k):
        for f in range(*GROUPS[k]):
            for i in range(4):
                sys_[r][f, 0, i] = gs[r][f, 1 + i, 0:1, :]
                sys_[r][f, 1, i] = gs[r][f, 1 + i, 31:32, :]

    def send_far(r, *fields):
        @pl.when(has_far)
        def _():
            for f in fields:
                halo_far(r, f).start()

    def send_near(r, k):
        halo_near(r, k).start()

    def send_y(r, *groups):
        @pl.when(has_left)
        def _():
            for k in groups:
                halo_y(r, k, 0).start()

        @pl.when(has_right)
        def _():
            for k in groups:
                halo_y(r, k, 1).start()

    def receive_near(r, k):
        halo_near(r, k).wait_recv()

        @pl.when(has_left)
        def _():
            halo_y(r, k, 1).wait_recv()

        @pl.when(has_right)
        def _():
            halo_y(r, k, 0).wait_recv()

    def receive_far(r, *fields):
        @pl.when(has_far)
        def _():
            for f in fields:
                halo_far(r, f).wait_recv()

    def first(f, i):
        fresh = plane(g0, hy0, f, i)
        g1[f, i] = fresh + 0.1 * g0[3, i] if f == 2 else fresh

    def second(f, i):
        fresh = plane(g1, hy1, f, i)
        gas_out[f, i - 1] = fresh + 0.1 * g1[3, i] if f == 2 else fresh

    def on_rest(todo):
        for n in range(3):
            todo(rest + n)

    loads = [
        pltpu.make_async_copy(gas_hbm.at[pl.ds(3, 1)], g0.at[pl.ds(3, 1), pl.ds(1, 4)], in_sem.at[0]),
        pltpu.make_async_copy(gas_hbm.at[pl.ds(0, 3)], g0.at[pl.ds(0, 3), pl.ds(1, 4)], in_sem.at[1]),
        pltpu.make_async_copy(gas_hbm.at[pl.ds(4, 1)], g0.at[pl.ds(4, 1), pl.ds(1, 4)], in_sem.at[2]),
        pltpu.make_async_copy(cell_hbm, cell.at[pl.ds(0, 128)], in_sem.at[3]),
        pltpu.make_async_copy(state_hbm, state, in_sem.at[4]),
        pltpu.make_async_copy(slot_hbm, slot, in_sem.at[5]),
        pltpu.make_async_copy(dest_hbm, dest, in_sem.at[6]),
        pltpu.make_async_copy(counts_hbm, counts, in_sem.at[7]),
    ]
    barrier = pltpu.get_barrier_semaphore()
    def greet(to):
        pl.semaphore_signal(barrier, inc=1, device_id=to, device_id_type=pl.DeviceIdType.MESH)

    greet(near)
    pl.when(has_far)(lambda: greet(far))
    pl.when(has_left)(lambda: greet(left))
    pl.when(has_right)(lambda: greet(right))
    for load in loads:
        load.start()

    @pl.when(edge)
    def _():
        for g in gs:
            for f in range(5):
                g[f, 5 * side] = jnp.zeros((32, 512), F32)

    @pl.when(c == 0)
    def _():
        for hy in hys:
            hy[:, 0] = jnp.zeros((5, 4, 1, 512), F32)

    @pl.when(c == nc - 1)
    def _():
        for hy in hys:
            hy[:, 1] = jnp.zeros((5, 4, 1, 512), F32)

    @pl.when(p == 0)
    def _():
        got[0] = jnp.zeros((4, 8, 256), F32)

    @pl.when(p == np_ - 1)
    def _():
        got[1] = jnp.zeros((4, 8, 256), F32)

    loads[0].wait()
    stage(0, 0)
    loads[1].wait()
    stage(0, 1)
    loads[2].wait()
    stage(0, 2)
    pl.semaphore_wait(barrier, 1 + has_far.astype(jnp.int32) + has_left.astype(jnp.int32) + has_right.astype(jnp.int32))
    send_y(0, 0)
    send_far(0, 3)
    send_near(0, 0)
    send_y(0, 1, 2)
    send_far(0, 0)
    send_near(0, 1)
    send_near(0, 2)
    acc[...] = jnp.zeros_like(acc)
    rel[...] = jnp.zeros_like(rel)
    for load in loads[3:]:
        load.wait()

    def on_blocks(rows, todo):
        def body(b, carry):
            todo(b, pl.ds(pl.multiple_of(b * rows, 8), rows))
            return carry
        lax.fori_loop(0, (160 if rows == 160 else 128) // rows, body, 0)

    def compact(b, ds):
        mass = state[pl.ds(pl.multiple_of(2 * ROWS * b, 8), ROWS, stride=2), :]
        temper = state[pl.ds(pl.multiple_of(2 * ROWS * b, 8) + 1, ROWS, stride=2), :]
        compact_block(b, ROWS, slot[ds, :], dest[ds, :], cell[ds, :], mass, temper, acc)
    on_blocks(ROWS, compact)
    turned = acc[...].T
    for f in range(4):
        head, tail = turned[32 * f:32 * f + 16, :], turned[32 * f + 16:32 * f + 32, :]
        both = head + tail if f < 2 else head * 256.0 + tail
        if f == 2:
            cell[128:144, :] = both[:, :128].astype(jnp.int32)
            cell[144:160, :] = both[:, 128:].astype(jnp.int32)
        elif f < 2:
            leaver[f, 0:16, :] = both[:, :128]
            leaver[f, 16:32, :] = both[:, 128:]
        else:
            box[0, 3] = both[:8]
            box[1, 3] = both[8:]

    receive_near(0, 0)
    first(3, 1 + 2 * near_half)
    first(3, 2 + 2 * near_half)
    stage_heat(near_half)
    send_heat_y(0)
    send_near(1, 0)
    send_far(0, 1, 2)
    first(3, 2 + side)
    receive_near(0, 1)

    def winds(i):
        for f in range(3):
            first(f, i)
    on_rest(winds)
    receive_far(0, 3)
    first(3, outer)
    stage_heat(far_half)
    send_heat_y(1)
    send_far(1, 3)
    send_far(0, 4)
    receive_near(0, 2)
    on_rest(lambda i: first(4, i))

    def second_heat(half):
        for n in range(2):
            i = n + 2 * half
            t2[i] = plane(g1, hy1, 3, i + 1)
        table(t2[pl.ds(2 * half, 2)].reshape(64, 512), tab)

    halo_near(1, 0).wait_recv()
    receive_heat_y(0)
    second_heat(near_half)

    def near_gather(b, ds):
        seen[ds, :] = gather_block(cell[ds, :], near_half, tab)
    on_blocks(160, near_gather)

    receive_far(0, 0, 1, 2)
    winds(outer)
    stage(1, 1)
    send_y(1, 1)
    send_far(1, 0, 1, 2)
    send_near(1, 1)
    receive_heat_y(1)
    receive_far(1, 3)
    second_heat(far_half)

    def far_gather(b, ds):
        seen[ds, :] += gather_block(cell[ds, :], far_half, tab)
    on_blocks(160, far_gather)
    left_over, warm, burned = burn(leaver[0], leaver[1], seen[128:160, :])
    place = lax.broadcasted_iota(jnp.int32, (8, 128), 0) * 256 + lax.broadcasted_iota(jnp.int32, (8, 128), 1)
    for face in range(2):
        for part in range(2):
            lanes = slice(128 * part, 128 * part + 128)
            live = place + 128 * part < counts[0, face]
            at = 16 * part + 8 * face
            for f, v in enumerate((left_over, warm, burned)):
                box[face, f, :, lanes] = jnp.where(live, v[at:at + 8], 0.0)
            box[face, 3, :, lanes] = jnp.where(live, box[face, 3, :, lanes], 0.0)
    down = remote(box.at[0], got.at[1], fs.at[0], fr.at[0], below)
    up = remote(box.at[1], got.at[0], fs.at[1], fr.at[1], above)
    pl.when(has_below)(down.start)
    pl.when(has_above)(up.start)
    receive_far(0, 4)
    first(4, outer)
    stage(1, 2)
    send_y(1, 2)
    send_far(1, 4)
    send_near(1, 2)
    left_over, warm, burned = burn(state[pl.ds(0, 128, stride=2), :], state[pl.ds(1, 128, stride=2), :], seen[0:128, :])
    state_out[pl.ds(0, 128, stride=2), :] = left_over
    state_out[pl.ds(1, 128, stride=2), :] = warm
    stay[...] = jnp.where(slot[...] < 0, burned, 0.0)

    def deposit(b, ds):
        rel[...] += deposit_block(dest[ds, :], stay[ds, :], 128)
        for f in range(2):
            for n in range(3):
                gas_out[f, rest + n - 1] = plane(g1, hy1, f, rest + n)
    receive_near(1, 1)
    on_blocks(128, deposit)


    on_rest(lambda i: second(2, i))
    receive_near(1, 2)
    on_rest(lambda i: second(4, i))
    for f in (0, 1, 2, 4):
        receive_far(1, f)
        second(f, outer)

    pl.when(has_below)(up.wait_recv)
    pl.when(has_above)(down.wait_recv)
    for d in range(2):
        for part in range(2):
            lanes = slice(128 * part, 128 * part + 128)
            at = 16 * d + 8 * part
            come[0, at:at + 8, :] = got[d, 2, :, lanes]
            come[1, at:at + 8, :] = got[d, 3, :, lanes]
            for f in range(3):
                arr_out[f, pl.ds(2 * part + d, 8, stride=4), :] = got[d, f, :, lanes]
    gas_out[3] = t2[...]

    @pl.when(has_far)
    def _():
        for r in range(2):
            for f in range(5):
                halo_far(r, f).wait_send()

    for r in range(2):
        for k in range(3):
            halo_near(r, k).wait_send()
    for d, there in ((0, has_left), (1, has_right)):
        @pl.when(there)
        def _():
            for r in range(2):
                for k in range(r, 3):
                    halo_y(r, k, d).wait_send()
                heat_y(r, d).wait_send()
    pl.when(has_below)(down.wait_send)
    pl.when(has_above)(up.wait_send)


def write_kernel(gas, state, arr, come, rel, gas_hbm, state_hbm, arr_hbm, last, sem):
    copies = [pltpu.make_async_copy(gas.at[f], gas_hbm.at[f], sem.at[f]) for f in range(3)]
    copies += [pltpu.make_async_copy(state, state_hbm, sem.at[5]), pltpu.make_async_copy(arr, arr_hbm, sem.at[6])]
    for copy in copies:
        copy.start()
    release = rel[...] + deposit_block(come[1].astype(jnp.int32), come[0], 32)
    both = release[:256, :] + release[256:, :]
    release = jnp.concatenate([both[:128], both[128:]], axis=1).reshape(4, 32, 512)
    for n in range(2):
        last[n] = gas[3 + n] + (1.5 * release if n == 0 else release)
        copies.append(pltpu.make_async_copy(last.at[n], gas_hbm.at[3 + n], sem.at[3 + n]))
        copies[-1].start()
    for copy in copies:
        copy.wait()


def on_device(gas, parcel_state, parcel_cell, parcel_dest, send_slot, face_counts):
    square = lambda a: a.reshape(128, 128)
    state = parcel_state.reshape(2, 128, 128).transpose(1, 0, 2).reshape(256, 128)
    vm = pl.BlockSpec(memory_space=pltpu.VMEM)
    hbm = pl.BlockSpec(memory_space=pltpu.HBM)
    i32 = lambda *s: pltpu.VMEM(s, jnp.int32)
    f32 = lambda *s: pltpu.VMEM(s, F32)
    dma = pltpu.SemaphoreType.DMA
    inputs = (gas, square(parcel_cell), square(parcel_dest), square(send_slot), state, face_counts.reshape(1, 2))
    results = pl.pallas_call(
        step_kernel,
        out_shape=(
            jax.ShapeDtypeStruct(gas.shape, F32),
            jax.ShapeDtypeStruct((256, 128), F32),
            jax.ShapeDtypeStruct((3, 32, 128), F32),
            jax.ShapeDtypeStruct((2, 32, 128), F32),
            jax.ShapeDtypeStruct((512, 256), F32),
        ),
        in_specs=[hbm] * 6,
        out_specs=(vm,) * 5,
        scratch_shapes=[
            f32(5, 6, 32, 512), f32(5, 6, 32, 512), f32(4, 32, 512),
            f32(5, 2, 4, 1, 512), f32(5, 2, 4, 1, 512), f32(5, 2, 4, 1, 512), f32(5, 2, 4, 1, 512),
            i32(160, 128), i32(128, 128), i32(128, 128), f32(256, 128), pltpu.SMEM((1, 2), jnp.int32),
            pltpu.VMEM((256, 256), BF), f32(160, 128), f32(2, 32, 128), f32(128, 128), f32(256, 128),
            f32(2, 4, 8, 256), f32(2, 4, 8, 256),
            dma((8,)), dma((2, 5)), dma((2, 5)), dma((2, 3)), dma((2, 3)), dma((2, 3, 2)), dma((2, 3, 2)), dma((2, 2)), dma((2, 2)), dma((2,)), dma((2,)),
        ],
        compiler_params=pltpu.CompilerParams(vmem_limit_bytes=44 << 20, collective_id=0, has_side_effects=True),
        name="dust_step",
    )(*[pltpu.with_memory_space_constraint(a, pltpu.HBM) for a in inputs])
    gas_out, out, arr = pl.pallas_call(
        write_kernel,
        out_shape=tuple(jax.ShapeDtypeStruct(a.shape, F32) for a in results[:3]),
        in_specs=[vm] * 5,
        out_specs=(hbm, hbm, hbm),
        scratch_shapes=[f32(2, 4, 32, 512), dma((7,))],
        compiler_params=pltpu.CompilerParams(vmem_limit_bytes=16 << 20),
        name="write",
    )(*[pltpu.with_memory_space_constraint(a, pltpu.VMEM) for a in results])
    parcels_out = out.reshape(128, 2, 128).transpose(1, 0, 2).reshape(2, 16384)
    arrivals = arr.reshape(3, 16, 2, 128).transpose(2, 0, 1, 3).reshape(2, 3, 2048)
    return (gas_out, parcels_out, arrivals)


def solution(mesh):
    in_specs = (
        P(None, "prop", "cross", None),
        P(None, ("prop", "cross")),
        P(("prop", "cross")),
        P(("prop", "cross")),
        P(("prop", "cross")),
        P("prop", "cross", None),
    )
    out_specs = (
        P(None, "prop", "cross", None),
        P(None, ("prop", "cross")),
        P(None, None, ("prop", "cross")),
    )
    return jax.shard_map(
        on_device, mesh=mesh, in_specs=in_specs, out_specs=out_specs, check_vma=False
    )
```
